128 devices in a mesh: dp: 8 (over z_hi, y), row: 4 (over z_lo, core), col: 4 (over x).
Axes of the slice: x: 4, y: 4, z: 4 (z_hi: 2, z_lo: 2; z = z_hi * 2 + z_lo), core: 2. Of those that a mesh axis runs over, the one named last changes fastest.
Arguments:
- tokens: bfloat16 [3072, 6144], P(('dp', 'row'), 'col'), may hold values from -6 to 6
- norm_scale_gain: float32 [6144], P('col'), may hold values from 0.1 to 1.9
- in_weight: bfloat16 [6144, 12288], P('col', 'row'), may hold values from -3 to 3
- out_weight: bfloat16 [12288, 6144], P('row', 'col'), may hold values from -0.0546875 to 0.0546875
- cotangent: bfloat16 [3072, 6144], P(('dp', 'row'), 'col'), may hold values from -6 to 6
Outputs:
- layer_output: bfloat16 [3072, 6144], P(('dp', 'row'), 'col')
- token_gradient: bfloat16 [3072, 6144], P(('dp', 'row'), 'col')
- gain_gradient: float32 [6144], P('col')
- grad_in_weight: bfloat16 [8, 768, 12288], P('dp', 'col', 'row')
- grad_out_weight: bfloat16 [8, 1536, 6144], P('dp', 'row', 'col')
The draws below stay inside these ranges and needn't reach their ends.
All inputs are finite; a program needn't handle non-finite values.
Results may differ from the reference program's by a relative error of at most 0.025.
Values may be sent and summed in bfloat16 or wider, within the bound.
A program may use at most 128 MiB of HBM per device.

```python
import jax
import jax.numpy as jnp
from jax import lax

MODEL_WIDTH = 6144
FF = 12288
TOK_DEV = 384
TOKENS = 3072
N_DP = 8
N_ROW = 4
N_COL = 4


def draw_in_weight(key, part):
    key = jax.random.fold_in(key, 11)
    noise_key = jax.random.fold_in(key, 1)
    common_key = jax.random.fold_in(key, 2)
    noise = jax.random.truncated_normal(noise_key, -4.0, 4.0, (MODEL_WIDTH, FF), jnp.float32)
    lowest = 0.3
    highest = 3.0
    common = jax.random.truncated_normal(common_key, -4.0, 4.0, (FF,), jnp.float32)
    position = jnp.arange(MODEL_WIDTH, dtype=jnp.float32) / MODEL_WIDTH
    profile = lowest * jnp.exp(position * jnp.log(highest / lowest))
    values = (noise + profile[:, None] * common[None, :]) / jnp.sqrt(jnp.float32(MODEL_WIDTH))
    return values.astype(jnp.bfloat16)


def steps_of(key, extent, split, smallest, high):
    def one(axis_at, shards_of):
        heights = jax.random.uniform(jax.random.fold_in(jax.random.fold_in(key, 6), axis_at), (shards_of,), jnp.float32, smallest / len(split), high / len(split))
        return jnp.repeat(jnp.exp(heights), extent[axis_at] // shards_of).reshape((-1,) + (1,) * (len(extent) - axis_at - 1))

    loudness = one(*split[0])
    for cut in split[1:]:
        loudness = loudness * one(*cut)
    return loudness


def centred(rng, shape, deviation, limit, pieces=(), kind=jnp.bfloat16):
    array = jax.random.normal(rng, shape, jnp.float32) * deviation
    if len(pieces) > 0:
        array = steps_of(rng, shape, pieces, -0.22, 0.18) * array
    return jnp.clip(array, min=-limit, max=limit).astype(kind)


def setup_inputs(seed: int = 0) -> dict:
    splits = jax.random.split(jax.random.key(seed), 6)
    tokens = centred(splits[0], (TOKENS, MODEL_WIDTH), 1.0, 6.0, ((0, 32), (1, 4)))
    norm_scale_gain = jnp.clip(1.0 + 0.18 * jax.random.normal(splits[1], (MODEL_WIDTH,), jnp.float32), 0.1, 1.9)
    in_weight = draw_in_weight(jax.random.fold_in(splits[5], 71), 0)
    out_weight = centred(splits[3], (FF, MODEL_WIDTH), FF ** -0.5, 0.0546875, ((0, 4), (1, 4)))
    cotangent = centred(splits[4], (TOKENS, MODEL_WIDTH), 1.0, 6.0, ((0, 32), (1, 4)))
    return {"tokens": tokens, "norm_scale_gain": norm_scale_gain, "in_weight": in_weight, "out_weight": out_weight, "cotangent": cotangent}


EPS = 1e-06

def gelu_slope(value):
    cdf = 0.5 * (1.0 + jax.scipy.special.erf(value * 0.7071067811865476))
    dens = jnp.exp(-0.5 * value * value) * 0.3989422804014327
    return cdf + value * dens

def reference(tokens, norm_scale_gain, in_weight, out_weight, cotangent):
    complete_input = tokens.astype(jnp.float32)
    input_mean = lax.optimization_barrier(jnp.mean(complete_input, axis=1, keepdims=True))
    second = lax.optimization_barrier(jnp.mean(complete_input * complete_input, axis=1, keepdims=True))
    inverse_deviation = lax.rsqrt(second - input_mean * input_mean + EPS)
    centered_input = (complete_input - input_mean) * inverse_deviation
    normed_tokens = (centered_input * norm_scale_gain).astype(jnp.bfloat16)
    pre = jnp.dot(normed_tokens, in_weight, preferred_element_type=jnp.float32)
    act = jax.nn.gelu(pre, approximate=False).astype(jnp.bfloat16)
    layer_output = (complete_input + jnp.dot(act, out_weight, preferred_element_type=jnp.float32)).astype(jnp.bfloat16)
    dact = jnp.dot(cotangent, out_weight.T, preferred_element_type=jnp.float32)
    dpre = (dact * gelu_slope(pre)).astype(jnp.bfloat16)
    normed_cotangent = jnp.dot(dpre, in_weight.T, preferred_element_type=jnp.float32)
    gain_gradient = lax.optimization_barrier(jnp.sum(normed_cotangent * centered_input, axis=0))
    centered_cotangent = normed_cotangent * norm_scale_gain
    token_gradient = (cotangent.astype(jnp.float32) + inverse_deviation * (centered_cotangent - lax.optimization_barrier(jnp.mean(centered_cotangent, axis=1, keepdims=True)) - centered_input * lax.optimization_barrier(jnp.mean(centered_cotangent * centered_input, axis=1, keepdims=True)))).astype(jnp.bfloat16)
    sum_in = jnp.zeros((MODEL_WIDTH, FF), jnp.float32)
    sum_out = jnp.zeros((FF, MODEL_WIDTH), jnp.float32)
    for group in range(N_DP):
        first_row = group * TOK_DEV
        normed_part = normed_tokens[first_row:first_row + TOK_DEV]
        dpre_part = dpre[first_row:first_row + TOK_DEV]
        act_part = act[first_row:first_row + TOK_DEV]
        cot_part = cotangent[first_row:first_row + TOK_DEV]
        term_in = lax.optimization_barrier(jnp.dot(normed_part.T, dpre_part, preferred_element_type=jnp.float32).astype(jnp.bfloat16))
        term_out = lax.optimization_barrier(jnp.dot(act_part.T, cot_part, preferred_element_type=jnp.float32).astype(jnp.bfloat16))
        sum_in = sum_in + term_in.astype(jnp.float32)
        sum_out = sum_out + term_out.astype(jnp.float32)
    grad_in_weight = sum_in.reshape(N_COL, N_DP, MODEL_WIDTH // (N_COL * N_DP), FF).transpose(1, 0, 2, 3).reshape(N_DP, MODEL_WIDTH // N_DP, FF).astype(jnp.bfloat16)
    grad_out_weight = sum_out.reshape(N_ROW, N_DP, FF // (N_ROW * N_DP), MODEL_WIDTH).transpose(1, 0, 2, 3).reshape(N_DP, FF // N_DP, MODEL_WIDTH).astype(jnp.bfloat16)
    return (layer_output, token_gradient, gain_gradient, grad_in_weight, grad_out_weight)
```

```python
import functools

import jax
import jax.numpy as jnp
from jax import lax
from jax.experimental import pallas as pl
from jax.experimental.pallas import tpu as pltpu
from jax.sharding import PartitionSpec as P

MODEL_WIDTH = 6144
EPS = 1e-06
MESH = pl.DeviceIdType.MESH
F32 = jnp.float32
BF16 = jnp.bfloat16

T = 96
G = 384
W = 1536
H = 1024
NC = 3
HALF = T // 2
FB = 192
LAST = (((1,), (1,)), ((), ()))
FIRST = (((0,), (0,)), ((), ()))


def rows(start, size, unit=16):
    return pl.ds(pl.multiple_of(start, unit), size)


def kernel(
    tok, gain, win_hbm, wout_hbm, cot,
    layer_out, token_grad, gain_grad, gin_out, gout_out,
    win, wout, nf, ngp, ngt, cg, ab, ag, dg, px, rx1, rx2, po, ro1, ro2,
    pgi, pgo, gi1, gi2, go1, go2, stat, tails, gains, wsem_in, wsem_out, osem, ssem, rsem,
):
    d, r, c = lax.axis_index("dp"), lax.axis_index("row"), lax.axis_index("col")
    zh, y = lax.div(d, 4), lax.rem(d, 4)
    zl, co = lax.div(r, 2), lax.rem(r, 2)
    cr, cl = lax.rem(c + 1, 4), lax.rem(c + 3, 4)
    yr, yl = lax.rem(y + 1, 4), lax.rem(y + 3, 4)
    cq, yq = lax.rem(c + 2, 4), lax.rem(y + 2, 4)
    XR, XL = (d, r, cr), (d, r, cl)
    YR, YL = (zh * 4 + yr, r, c), (zh * 4 + yl, r, c)
    ZL, ZH = (d, (1 - zl) * 2 + co, c), ((1 - zh) * 4 + y, r, c)
    CO = (d, zl * 2 + 1 - co, c)
    XA = (d, r, c + 1 - 2 * lax.rem(c, 2))
    XB = (d, r, 3 - c)
    YA = (zh * 4 + y + 1 - 2 * lax.rem(y, 2), r, c)
    YB = (zh * 4 + 3 - y, r, c)
    zr = (1 - zl) * 2 + co
    zc = (1 - zl) * 2 + 1 - co

    count = [0]
    sends = []

    def rc(src, dst, dev):
        i = count[0]
        count[0] += 1
        cp = pltpu.make_async_remote_copy(
            src, dst, ssem.at[i], rsem.at[i], device_id=dev, device_id_type=MESH
        )
        cp.start()
        sends.append(cp)
        return cp

    def drain(cps):
        for cp in cps:
            cp.wait_send()
        gone = [id(cp) for cp in cps]
        sends[:] = [cp for cp in sends if id(cp) not in gone]

    def win_copy(j, k):
        return pltpu.make_async_copy(
            win_hbm.at[:, rows(k * 384 + j * 128, 128, 128)],
            win.at[j, :, rows(k * 128, 128, 128)],
            wsem_in.at[j, k],
        )

    def wout_copy(j, k):
        return pltpu.make_async_copy(
            wout_hbm.at[rows(k * 384 + j * 128, 128, 128)],
            wout.at[j, rows(k * 128, 128, 128)],
            wsem_out.at[j, k],
        )

    for j in range(NC):

        @pl.loop(0, 8)
        def _(k):
            wout_copy(j, k).start()
            win_copy(j, k).start()

    def wait_wout(j):
        @pl.loop(0, 8)
        def _(k):
            wout_copy(j, k).wait()

    def wait_win(j):
        @pl.loop(0, 8)
        def _(k):
            win_copy(j, k).wait()

    barrier = pltpu.get_barrier_semaphore()
    for dev in (XR, XL, YR, YL, ZL, ZH, CO):
        pl.semaphore_signal(barrier, inc=1, device_id=dev, device_id_type=MESH)

    cg[rows(r * T, T)] = cot[...]
    x = tok[...].astype(F32)
    lane = lax.broadcasted_iota(jnp.int32, (T, 128), 1)

    def two(a, b):
        return jnp.where(lane == 0, a, jnp.where(lane == 1, b, 0.0))

    stat[0] = two(jnp.sum(x, axis=1, keepdims=True), jnp.sum(x * x, axis=1, keepdims=True))
    pl.semaphore_wait(barrier, 7)

    sa = rc(stat.at[0], stat.at[1], XA)

    def gather_row(ref, base, width=None):
        own = ref.at[rows(base + r * T, T)]
        return [rc(own, own, CO), rc(own, own, ZL)]

    def gather_row_forward(ref, base, cps):
        cps[1].wait_recv()
        blk = ref.at[rows(base + zr * T, T)]
        cps.append(rc(blk, blk, CO))

    def gather_row_end(cps):
        cps[0].wait_recv()
        cps[2].wait_recv()

    cot_g = gather_row(cg, 0)
    sa.wait_recv()
    stat[2] = stat[0] + stat[1]
    sb = rc(stat.at[2], stat.at[3], XB)
    sb.wait_recv()
    stat[4] = stat[2] + stat[3]
    mean = stat[4, :, 0:1] / MODEL_WIDTH
    inverse = lax.rsqrt(stat[4, :, 1:2] / MODEL_WIDTH - mean * mean + EPS)
    nf[rows(r * T, T)] = ((tok[...].astype(F32) - mean) * inverse * gain[...]).astype(BF16)
    nor_g = gather_row(nf, 0)
    gather_row_forward(cg, 0, cot_g)
    gather_row_end(cot_g)

    cot_h = rc(cot, cg.at[rows(G + r * T, T)], ZH)
    nor_h = rc(
        nf.at[rows(r * T, T), rows((1 - zh) * 768, 768, 128)], ngp.at[rows(r * T, T)], ZH
    )

    s1, s2 = {}, {}

    def ring_first(part, buf1, size, me_o, right, left, blk):
        h = size // 2
        return [
            rc(part.at[rows(me_o * size, h)], buf1.at[0], right),
            rc(part.at[rows(me_o * size + h, h)], buf1.at[1], left),
        ]

    def ring_second(part, buf1, buf2, size, ir, il, right, left, cps):
        h = size // 2
        cps[0].wait_recv()
        a = rows(ir * size, h)
        part[a] = (part[a].astype(F32) + buf1[0].astype(F32)).astype(BF16)
        one = rc(part.at[rows(ir * size, size)], buf2.at[0], right)
        cps[1].wait_recv()
        b = rows(il * size + h, h)
        part[b] = (part[b].astype(F32) + buf1[1].astype(F32)).astype(BF16)
        other = rc(part.at[rows(il * size, size)], buf2.at[1], left)
        return [one, other]

    def dact_part(j):
        wait_wout(j)

        @pl.loop(0, H // 256)
        def _(n):
            px[0, j % 2, :, rows(n * 256, 256, 256)] = lax.dot_general(
                cg[0:G], wout[j, rows(n * 256, 256)], LAST, preferred_element_type=F32
            ).astype(BF16)

        s1[0, j] = ring_first(px.at[0, j % 2], rx1.at[0, j], T, cq, XR, XL, None)

    def pre_part(j):
        wait_win(j)

        @pl.loop(0, H // 256)
        def _(n):
            px[1, j % 2, :, rows(n * 256, 256, 256)] = jnp.dot(
                nf[...], win[j, :, rows(n * 256, 256, 256)], preferred_element_type=F32
            ).astype(BF16)

        s1[1, j] = ring_first(px.at[1, j % 2], rx1.at[1, j], T, cq, XR, XL, None)

    def rs_second(kind, j):
        s2[kind, j] = ring_second(
            px.at[kind, j % 2], rx1.at[kind, j], rx2.at[kind, j], T, cr, cl, XR, XL, s1[kind, j]
        )

    gat = {}

    def gather_x(key, ref, base):
        own = ref.at[rows(base + c * T, T)]
        gat[key] = [rc(own, own, XR), rc(own, own, XL)]

    def gather_x_forward(key, ref, base):
        cps = gat[key]
        cps[0].wait_recv()
        a = ref.at[rows(base + cl * T, HALF)]
        cps.append(rc(a, a, XR))
        cps[1].wait_recv()
        b = ref.at[rows(base + cr * T + HALF, HALF)]
        cps.append(rc(b, b, XL))

    def gather_x_end(key):
        gat[key][2].wait_recv()
        gat[key][3].wait_recv()

    zsend = {}

    def activate(j):
        for kind in (0, 1):
            for cp in s2[kind, j]:
                cp.wait_recv()

        @pl.loop(0, H // 256)
        def _(n):
            at = rows(n * 256, 256, 256)
            own = rows(c * T, T)
            dact = (
                px[0, j % 2, own, at].astype(F32)
                + rx2[0, j, 0, :, at].astype(F32)
                + rx2[0, j, 1, :, at].astype(F32)
            )
            pre = (
                px[1, j % 2, own, at].astype(F32)
                + rx2[1, j, 0, :, at].astype(F32)
                + rx2[1, j, 1, :, at].astype(F32)
            )
            cdf = 0.5 * (1.0 + lax.erf(pre * 0.7071067811865476))
            dens = jnp.exp(-0.5 * pre * pre) * 0.3989422804014327
            ab[j, own, at] = (pre * cdf).astype(BF16)
            dg[j, own, at] = (dact * (cdf + pre * dens)).astype(BF16)

        gather_x(("a", j), ab.at[j], 0)
        gather_x(("d", j), dg.at[j], 0)
        zsend["a", j] = rc(
            ab.at[j, rows(c * T, T), rows((1 - zh) * 512, 512, 128)],
            ag.at[j, rows(G + c * T, T)],
            ZH,
        )
        zsend["d", j] = rc(dg.at[j, rows(c * T, T)], dg.at[j, rows(G + c * T, T)], ZH)

    def gather_forward(j):
        gather_x_forward(("a", j), ab.at[j], 0)
        gather_x_forward(("d", j), dg.at[j], 0)
        zsend["a", j].wait_recv()
        gather_x(("ap", j), ag.at[j], G)
        zsend["d", j].wait_recv()
        gather_x(("dp", j), dg.at[j], G)

    def partner_forward(j):
        gather_x_forward(("ap", j), ag.at[j], G)
        gather_x_forward(("dp", j), dg.at[j], G)

    y1, y2 = {}, {}

    def grad_out_part(j):
        gather_x_end(("a", j))
        ag[j, 0:G] = ab[j, :, rows(zh * 512, 512, 128)]
        gather_x_end(("ap", j))
        if j >= 2:
            drain(y1["o", j - 2] + y2["o", j - 2])
        part = pgo.at[j % 2]

        def block(b):
            at = rows(b * 128, 128, 128)
            part[at] = lax.dot_general(
                ag[j, :, at], cg[...], FIRST, preferred_element_type=F32
            ).astype(BF16)

        block(yq)
        y1["o", j] = ring_first(part, go1.at[j], 128, yq, YR, YL, None)

        @pl.loop(1, 4)
        def _(i):
            block(lax.rem(yq + i, 4))

    def grad_in_part(j):
        gather_x_end(("d", j))
        gather_x_end(("dp", j))
        if j >= 2:
            drain(y1["i", j - 2] + y2["i", j - 2])
        part = pgi.at[j % 2]

        def block(b):
            at = rows(b * FB, FB)
            part[at] = jnp.dot(ngt[at], dg[j], preferred_element_type=F32).astype(BF16)

        block(yq)
        y1["i", j] = ring_first(part, gi1.at[j], FB, yq, YR, YL, None)

        @pl.loop(1, 4)
        def _(i):
            block(lax.rem(yq + i, 4))

    def grad_second(key, j):
        if key == "o":
            y2["o", j] = ring_second(
                pgo.at[j % 2], go1.at[j], go2.at[j], 128, yr, yl, YR, YL, y1["o", j]
            )
        else:
            y2["i", j] = ring_second(
                pgi.at[j % 2], gi1.at[j], gi2.at[j], FB, yr, yl, YR, YL, y1["i", j]
            )

    ocps = []

    def grad_end(key, j):
        for cp in y2[key, j]:
            cp.wait_recv()
        part, buf, size, out = (
            (pgo, go2, 128, gout_out) if key == "o" else (pgi, gi2, FB, gin_out)
        )
        own = rows(y * size, size)
        buf[j, 0] = (
            part[j % 2, own].astype(F32) + buf[j, 0].astype(F32) + buf[j, 1].astype(F32)
        ).astype(BF16)
        cp = pltpu.make_async_copy(
            buf.at[j, 0], out.at[j], osem.at[0 if key == "o" else 1, j]
        )
        cp.start()
        ocps.append(cp)

    dact_part(0)
    gather_row_forward(nf, 0, nor_g)
    gather_row_end(nor_g)
    pre_part(0)
    rs_second(0, 0)
    rs_second(1, 0)
    dact_part(1)
    pre_part(1)
    activate(0)
    cot_h.wait_recv()
    cot_pg = gather_row(cg, G)
    nor_h.wait_recv()
    nor_pg = gather_row(ngp, 0)
    rs_second(0, 1)
    rs_second(1, 1)
    gather_forward(0)
    drain(s1[0, 0] + s2[0, 0])
    dact_part(2)
    drain(s1[1, 0] + s2[1, 0])
    pre_part(2)
    ngt[:, 0:G] = jnp.transpose(nf[:, rows(zh * 768, 768, 128)])
    gather_row_forward(cg, G, cot_pg)
    gather_row_forward(ngp, 0, nor_pg)
    activate(1)
    gather_row_end(cot_pg)
    gather_row_end(nor_pg)
    ngt[:, G:] = jnp.transpose(ngp[...])
    partner_forward(0)
    rs_second(0, 2)
    rs_second(1, 2)
    gather_forward(1)
    grad_out_part(0)
    activate(2)
    grad_in_part(0)
    partner_forward(1)
    gather_forward(2)
    grad_second("o", 0)
    grad_second("i", 0)
    grad_out_part(1)
    grad_in_part(1)
    partner_forward(2)
    grad_end("o", 0)
    grad_second("o", 1)
    grad_end("i", 0)
    grad_second("i", 1)
    grad_out_part(2)
    grad_in_part(2)

    def row_first(q):
        return [
            rc(po.at[q, rows((z * 2 + 1 - co) * T, T)], ro1.at[q, z], CO) for z in (0, 1)
        ]

    def row_second(q, cps):
        for z in (0, 1):
            cps[z].wait_recv()
            at = rows((z * 2 + co) * T, T)
            po[q, at] = (po[q, at].astype(F32) + ro1[q, z].astype(F32)).astype(BF16)
        return rc(po.at[q, rows(zr * T, T)], ro2.at[q], ZL)

    @pl.loop(0, W // 256)
    def _(n):
        at = rows(n * 256, 256, 256)
        total = lax.dot_general(dg[0, 0:G], win[0, at], LAST, preferred_element_type=F32)
        for j in range(1, NC):
            total += lax.dot_general(dg[j, 0:G], win[j, at], LAST, preferred_element_type=F32)
        po[1, :, at] = total.astype(BF16)

    dn1 = row_first(1)

    @pl.loop(0, W // 256)
    def _(n):
        at = rows(n * 256, 256, 256)
        total = jnp.dot(ab[0], wout[0, :, at], preferred_element_type=F32)
        for j in range(1, NC):
            total += jnp.dot(ab[j], wout[j, :, at], preferred_element_type=F32)
        po[0, :, at] = total.astype(BF16)

    lo1 = row_first(0)
    dn2 = row_second(1, dn1)
    lo2 = row_second(0, lo1)
    grad_end("o", 1)
    grad_second("o", 2)
    grad_end("i", 1)
    grad_second("i", 2)

    dn2.wait_recv()
    own = rows(r * T, T)
    mean = stat[4, :, 0:1] / MODEL_WIDTH
    inverse = lax.rsqrt(stat[4, :, 1:2] / MODEL_WIDTH - mean * mean + EPS)
    dnorm = po[1, own].astype(F32) + ro2[1].astype(F32)
    xhat = (tok[...].astype(F32) - mean) * inverse
    gains[0] = jnp.sum((dnorm * xhat).reshape(T // 8, 8, W), axis=0)
    ga = rc(gains.at[0], gains.at[1], CO)
    dxhat = dnorm * gain[...]
    tails[0] = two(
        jnp.sum(dxhat, axis=1, keepdims=True), jnp.sum(dxhat * xhat, axis=1, keepdims=True)
    )
    ta = rc(tails.at[0], tails.at[1], XA)
    ta.wait_recv()
    tails[2] = tails[0] + tails[1]
    tb = rc(tails.at[2], tails.at[3], XB)
    ga.wait_recv()
    gains[2] = gains[0] + gains[1]
    gb = rc(gains.at[2], gains.at[3], ZL)
    tb.wait_recv()
    tails[4] = tails[2] + tails[3]
    first = tails[4, :, 0:1] / MODEL_WIDTH
    second = tails[4, :, 1:2] / MODEL_WIDTH
    dnorm = po[1, own].astype(F32) + ro2[1].astype(F32)
    xhat = (tok[...].astype(F32) - mean) * inverse
    token_grad[...] = (
        cot[...].astype(F32) + inverse * (dnorm * gain[...] - first - xhat * second)
    ).astype(BF16)
    gb.wait_recv()
    gains[4] = gains[2] + gains[3]
    gc = rc(gains.at[4], gains.at[5], ZH)
    lo2.wait_recv()
    layer_out[...] = (
        tok[...].astype(F32) + (po[0, own].astype(F32) + ro2[0].astype(F32))
    ).astype(BF16)
    gc.wait_recv()
    gains[6] = gains[4] + gains[5]
    gd = rc(gains.at[6], gains.at[7], YA)
    gd.wait_recv()
    gains[8] = gains[6] + gains[7]
    ge = rc(gains.at[8], gains.at[9], YB)
    ge.wait_recv()
    gain_grad[...] = jnp.sum(gains[8] + gains[9], axis=0, keepdims=True)
    grad_end("o", 2)
    grad_end("i", 2)
    drain(list(sends))
    for cp in ocps:
        cp.wait()
    assert count[0] == N_COPIES, count[0]


N_COPIES = 131


def body(tokens, norm_scale_gain, in_weight, out_weight, cotangent):
    vm = pl.BlockSpec(memory_space=pltpu.VMEM)
    hbm = pl.BlockSpec(memory_space=pl.ANY)
    layer_out, token_grad, gain_grad, gin, gout = pl.pallas_call(
        kernel,
        out_shape=(
            jax.ShapeDtypeStruct((T, W), BF16),
            jax.ShapeDtypeStruct((T, W), BF16),
            jax.ShapeDtypeStruct((1, W), F32),
            jax.ShapeDtypeStruct((NC, FB, H), BF16),
            jax.ShapeDtypeStruct((NC, 128, W), BF16),
        ),
        in_specs=[vm, vm, hbm, hbm, vm],
        out_specs=(vm, vm, vm, hbm, hbm),
        scratch_shapes=[
            pltpu.VMEM((NC, W, H), BF16),
            pltpu.VMEM((NC, H, W), BF16),
            pltpu.VMEM((G, W), BF16),
            pltpu.VMEM((G, 768), BF16),
            pltpu.VMEM((768, 2 * G), BF16),
            pltpu.VMEM((2 * G, W), BF16),
            pltpu.VMEM((NC, G, H), BF16),
            pltpu.VMEM((NC, 2 * G, 512), BF16),
            pltpu.VMEM((NC, 2 * G, H), BF16),
            pltpu.VMEM((2, 2, G, H), BF16),
            pltpu.VMEM((2, NC, 2, HALF, H), BF16),
            pltpu.VMEM((2, NC, 2, T, H), BF16),
            pltpu.VMEM((2, G, W), BF16),
            pltpu.VMEM((2, 2, T, W), BF16),
            pltpu.VMEM((2, T, W), BF16),
            pltpu.VMEM((2, 768, H), BF16),
            pltpu.VMEM((2, 512, W), BF16),
            pltpu.VMEM((NC, 2, FB // 2, H), BF16),
            pltpu.VMEM((NC, 2, FB, H), BF16),
            pltpu.VMEM((NC, 2, 64, W), BF16),
            pltpu.VMEM((NC, 2, 128, W), BF16),
            pltpu.VMEM((5, T, 128), F32),
            pltpu.VMEM((5, T, 128), F32),
            pltpu.VMEM((10, 8, W), F32),
            pltpu.SemaphoreType.DMA((NC, 8)),
            pltpu.SemaphoreType.DMA((NC, 8)),
            pltpu.SemaphoreType.DMA((2, NC)),
            pltpu.SemaphoreType.DMA((N_COPIES,)),
            pltpu.SemaphoreType.DMA((N_COPIES,)),
        ],
        compiler_params=pltpu.CompilerParams(
            collective_id=0, has_side_effects=True, vmem_limit_bytes=62 * 2**20
        ),
        cost_estimate=pl.CostEstimate(
            flops=22 * 10**9, bytes_accessed=24 * 10**6, transcendentals=600000
        ),
        name="feed_forward",
    )(tokens, norm_scale_gain.reshape(1, W), in_weight, out_weight, cotangent)
    grad_in = gin.reshape(NC, FB, 8, 128).transpose(1, 2, 0, 3).reshape(1, FB, NC * H)
    grad_out = gout.reshape(1, NC * 128, W)
    return (layer_out, token_grad, gain_grad.reshape(W), grad_in, grad_out)


def solution(mesh):
    in_specs = (
        P(("dp", "row"), "col"),
        P("col"),
        P("col", "row"),
        P("row", "col"),
        P(("dp", "row"), "col"),
    )
    out_specs = (
        P(("dp", "row"), "col"),
        P(("dp", "row"), "col"),
        P("col"),
        P("dp", "col", "row"),
        P("dp", "row", "col"),
    )
    return jax.shard_map(body, mesh=mesh, in_specs=in_specs, out_specs=out_specs, check_vma=False)
```

```python
import jax
import jax.numpy as jnp
from jax import lax
from jax.experimental import pallas as pl
from jax.experimental.pallas import tpu as pltpu
from jax.sharding import PartitionSpec as P

MODEL_WIDTH = 6144
EPS = 1e-06
MESH = pl.DeviceIdType.MESH
F32 = jnp.float32
BF16 = jnp.bfloat16

T = 96
G = 384
W = 1536
H = 1024
NC = 3
HALF = T // 2
FB = 192
FG = 4 * FB
LAST = (((1,), (1,)), ((), ()))
FIRST = (((0,), (0,)), ((), ()))

ACT_WAY = (2, 2, 2)
DPRE_WAY = (2, 2, 2)
SPLIT_DACT = (0, 1)
SPLIT_PRE = (0,)
SPLIT_IN = (2,)
SPLIT_OUT = ()

ORDER = (
    "cotg", "st1", "dact1a", "st2", "dact0a", "rsd1a", "st3", "coth", "rsd0a", "cotf", "dact1b",
    "dact0b", "pre0a", "rsd1b", "norf", "rsd0b", "pre0b", "rsp0a", "pre1", "cph", "rsp0b", "rsp1",
    "norh", "act0", "dact2", "af0", "cpf", "sd0", "za0", "nph", "ap0", "act1", "npf", "zaq0",
    "ngt0", "df0", "zd0", "sd1", "go0", "pre2", "zdq0", "dp0", "ngt1", "gso0", "af1", "zd1", "df1",
    "rsp2", "rsd2", "gi0", "za1", "ap1", "dp1", "gsi0", "zaq1", "zdq1", "act2", "go1", "za2",
    "zd2", "gi1", "sd2", "gso1", "dna", "gsi1", "af2", "geo0", "df2", "zaq2", "ap2", "dnb", "go2",
    "dp2", "zdq2", "dn2", "out", "gei0", "gei1", "gi2", "gso2", "gsi2a", "fin", "gb", "gc", "lo2",
    "gd", "geo1", "gsi2b", "t2", "geo2", "lo3", "gei2a", "ge", "t3", "gei2b", "gz",
)


def rows(start, size, unit=16):
    return pl.ds(pl.multiple_of(start, unit), size)


def kernel(
    tok, gain, win_hbm, wout_hbm, cot,
    layer_out, token_grad, gain_grad, gin_out, gout_out,
    win, wout, nf, ngp, ngt, cg, ab, ag, dg, px, rx1, rx2, po, ro1, ro2, acc,
    pgi, pgo, gi1, gi2, go1, go2, stat, tails, gains, wsem_in, wsem_out, osem, ssem, rsem,
):
    d, r, c = lax.axis_index("dp"), lax.axis_index("row"), lax.axis_index("col")
    zh, y = lax.div(d, 4), lax.rem(d, 4)
    zl, co = lax.div(r, 2), lax.rem(r, 2)
    cr, cl = lax.rem(c + 1, 4), lax.rem(c + 3, 4)
    yr, yl = lax.rem(y + 1, 4), lax.rem(y + 3, 4)
    cq, yq = lax.rem(c + 2, 4), lax.rem(y + 2, 4)
    XR, XL = (d, r, cr), (d, r, cl)
    YR, YL = (zh * 4 + yr, r, c), (zh * 4 + yl, r, c)
    ZL, ZH = (d, (1 - zl) * 2 + co, c), ((1 - zh) * 4 + y, r, c)
    CO = (d, zl * 2 + 1 - co, c)
    XA = (d, r, c + 1 - 2 * lax.rem(c, 2))
    XB = (d, r, 3 - c)
    YA = (zh * 4 + y + 1 - 2 * lax.rem(y, 2), r, c)
    YB = (zh * 4 + 3 - y, r, c)

    def slot(ref, i, first=0):
        return ref.at[pl.ds(first + 2 * (i % 2), 2), i // 2]

    count = [0]
    sends = []
    V = {}

    def rc(src, dst, dev):
        i = count[0]
        count[0] += 1
        cp = pltpu.make_async_remote_copy(
            src, dst, ssem.at[i], rsem.at[i], device_id=dev, device_id_type=MESH
        )
        cp.start()
        sends.append(cp)
        return cp

    def recv(*cps):
        for cp in cps:
            cp.wait_recv()

    def drain(cps):
        for cp in cps:
            cp.wait_send()
        gone = [id(cp) for cp in cps]
        sends[:] = [cp for cp in sends if id(cp) not in gone]

    def win_copy(j, k):
        return pltpu.make_async_copy(
            win_hbm.at[:, rows(k * 384 + j * 128, 128, 128)],
            win.at[j, :, rows(k * 128, 128, 128)],
            wsem_in.at[j, k],
        )

    def wout_copy(j, k):
        return pltpu.make_async_copy(
            wout_hbm.at[rows(k * 384 + j * 128, 128, 128)],
            wout.at[j, rows(k * 128, 128, 128)],
            wsem_out.at[j, k],
        )

    for j in range(NC):

        @pl.loop(0, 8)
        def _(k):
            wout_copy(j, k).start()
            win_copy(j, k).start()

    loaded = []

    def need(copy, key, j):
        if (key, j) not in loaded:
            loaded.append((key, j))

            @pl.loop(0, 8)
            def _(k):
                copy(j, k).wait()

    barrier = pltpu.get_barrier_semaphore()
    for dev in (XR, XL, YR, YL, ZL, ZH, CO):
        pl.semaphore_signal(barrier, inc=1, device_id=dev, device_id_type=MESH)

    cg[0:2, 0] = cot[...].reshape(2, HALF, W)
    x = tok[...].astype(F32)
    lane = lax.broadcasted_iota(jnp.int32, (T, 128), 1)

    def two(a, b):
        return jnp.where(lane == 0, a, jnp.where(lane == 1, b, 0.0))

    stat[0] = two(jnp.sum(x, axis=1, keepdims=True), jnp.sum(x * x, axis=1, keepdims=True))
    pl.semaphore_wait(barrier, 7)

    def mean_inverse():
        mean = stat[4, :, 0:1] / MODEL_WIDTH
        return mean, lax.rsqrt(stat[4, :, 1:2] / MODEL_WIDTH - mean * mean + EPS)

    S = {}

    def spread(key, ref, first=0):
        own = slot(ref, 0, first)
        V[key] = [rc(own, slot(ref, 1, first), CO), rc(own, slot(ref, 2, first), ZL)]

    def spread_on(key, ref, first=0):
        recv(V[key][1])
        V[key].append(rc(slot(ref, 2, first), slot(ref, 3, first), CO))

    done = []

    def once(key, *cps):
        if key not in done:
            done.append(key)
            recv(*cps)

    def own_chip(key):
        once(key + "0", V[key][0])

    def whole(key):
        own_chip(key)
        once(key + "1", V[key][2])

    S["cotg"] = lambda: spread("cot", cg)
    S["cotf"] = lambda: spread_on("cot", cg)

    def st1():
        V["sa"] = rc(stat.at[0], stat.at[1], XA)

    def st2():
        recv(V["sa"])
        stat[2] = stat[0] + stat[1]
        V["sb"] = rc(stat.at[2], stat.at[3], XB)

    def st3():
        recv(V["sb"])
        stat[4] = stat[2] + stat[3]
        mean, inverse = mean_inverse()
        normed = ((tok[...].astype(F32) - mean) * inverse * gain[...]).astype(BF16)
        nf[0:2, 0] = normed.reshape(2, HALF, W)
        spread("nor", nf)

    S["st1"], S["st2"], S["st3"] = st1, st2, st3
    S["norf"] = lambda: spread_on("nor", nf)

    def coth():
        V["coth"] = rc(slot(cg, 0), slot(cg, 0, 4), ZH)

    def norh():
        V["norh"] = rc(
            nf.at[0:2, 0, :, rows((1 - zh) * FG, FG, 128)], slot(ngp, 0), ZH
        )

    def cph():
        recv(V["coth"])
        spread("cp", cg, 4)

    def nph():
        recv(V["norh"])
        spread("np", ngp)

    def ngt0():
        whole("nor")
        ngt[:, 0:G] = jnp.transpose(nf[:, :, :, rows(zh * FG, FG, 128)].reshape(G, FG))

    def ngt1():
        whole("np")
        ngt[:, G:] = jnp.transpose(ngp[...].reshape(G, FG))

    S["coth"], S["norh"], S["cph"], S["nph"] = coth, norh, cph, nph
    S["ngt0"], S["ngt1"] = ngt0, ngt1
    S["cpf"] = lambda: spread_on("cp", cg, 4)
    S["npf"] = lambda: spread_on("np", ngp)

    def add(part, buf):
        part[...] = (part[...].astype(F32) + buf[...].astype(F32)).astype(BF16)

    CA, CB = pl.ds(0, H // 2), pl.ds(H // 2, H // 2)

    def product(kind, j, h):
        key = "cot" if kind == 0 else "nor"
        (need(wout_copy, "o", j) if kind == 0 else need(win_copy, "i", j))
        own_chip(key) if h == 0 else whole(key)
        if j >= 2 and h != 1:
            drain(V["x1", kind, j - 2] + V["x2", kind, j - 2])
        src = cg if kind == 0 else nf
        part = px.at[kind, j % 2]

        @pl.loop(0, H // 256)
        def _(n):
            at = rows(n * 256, 256, 256)
            if h is None:
                left = src[0:4].reshape(G, W)
            else:
                left = src[0:4, h].reshape(G // 2, W)
            if kind == 0:
                out = lax.dot_general(left, wout[j, at], LAST, preferred_element_type=F32)
            else:
                out = jnp.dot(left, win[j, :, at], preferred_element_type=F32)
            if h is None:
                part[:, :, :, at] = out.astype(BF16).reshape(4, 2, HALF, 256)
            else:
                part[:, h, :, at] = out.astype(BF16).reshape(4, HALF, 256)

        buf = rx1.at[kind, j]
        if h is None:
            new = [rc(part.at[cq, 0], buf.at[0], XR), rc(part.at[cq, 1], buf.at[1], XL)]
        else:
            new = [
                rc(part.at[cq, h, :, CA], buf.at[h, :, CA], XR),
                rc(part.at[cq, h, :, CB], buf.at[h, :, CB], XL),
            ]
        V["x1", kind, j, h] = new
        V["x1", kind, j] = V.get(("x1", kind, j), []) + new

    def second(kind, j, h):
        one, other = V["x1", kind, j, h]
        part, buf, out = px.at[kind, j % 2], rx1.at[kind, j], rx2.at[kind, j]
        new = []
        if h is None:
            recv(one)
            add(part.at[cr, 0], buf.at[0])
            new.append(rc(part.at[cr], out.at[0], XR))
            recv(other)
            add(part.at[cl, 1], buf.at[1])
            new.append(rc(part.at[cl], out.at[1], XL))
        else:
            recv(one)
            add(part.at[cr, h, :, CA], buf.at[h, :, CA])
            new.append(rc(part.at[cr, h], out.at[0, h], XR))
            recv(other)
            add(part.at[cl, h, :, CB], buf.at[h, :, CB])
            new.append(rc(part.at[cl, h], out.at[1, h], XL))
        V["x2", kind, j] = V.get(("x2", kind, j), []) + new

    def activate(j):
        recv(*V["x2", 0, j], *V["x2", 1, j])

        @pl.loop(0, H // 256)
        def _(n):
            at = rows(n * 256, 256, 256)

            def total(kind):
                return (
                    px[kind, j % 2, c, :, :, at].astype(F32)
                    + rx2[kind, j, 0, :, :, at].astype(F32)
                    + rx2[kind, j, 1, :, :, at].astype(F32)
                ).reshape(T, 256)

            dact, pre = total(0), total(1)
            cdf = 0.5 * (1.0 + lax.erf(pre * 0.7071067811865476))
            dens = jnp.exp(-0.5 * pre * pre) * 0.3989422804014327
            ab[j, rows(c * T, T), at] = (pre * cdf).astype(BF16)
            dg[j, rows(c * T, T), at] = (dact * (cdf + pre * dens)).astype(BF16)

        both_ways(("a", j), ab.at[j], 0)

    def both_ways(key, ref, base):
        own = ref.at[rows(base + c * T, T)]
        V[key] = [rc(own, own, XR), rc(own, own, XL)]

    def forward(key, ref, base):
        one, other = V[key]
        once((key, 0), one)
        a = ref.at[rows(base + cl * T, HALF)]
        V[key].append(rc(a, a, XR))
        once((key, 1), other)
        b = ref.at[rows(base + cr * T + HALF, HALF)]
        V[key].append(rc(b, b, XL))

    def ends(key):
        once((key, 2), V[key][2])
        once((key, 3), V[key][3])

    def over_z(kind, j, piece):
        if kind == "a":
            return rc(
                ab.at[j, rows(piece * T, T), rows((1 - zh) * 512, 512, 128)],
                ag.at[j, rows(G + piece * T, T)],
                ZH,
            )
        return rc(dg.at[j, rows(piece * T, T)], dg.at[j, rows(G + piece * T, T)], ZH)

    def partner_steps(kind, j, way):
        ref = ag if kind == "a" else dg
        key = (kind + "p", j)
        name = "z%s%s%d"

        def z_own():
            V["z", kind, j] = over_z(kind, j, c)

        S["z%s%d" % (kind, j)] = z_own

        def over_x():
            once(("z", kind, j), V["z", kind, j])
            both_ways(key, ref.at[j], G)

        def opposite():
            ends((kind, j))
            V["zq", kind, j] = over_z(kind, j, cq)

        def neighbours():
            once(((kind, j), 0), V[kind, j][0])
            once(((kind, j), 1), V[kind, j][1])
            V["zn", kind, j] = [over_z(kind, j, cl), over_z(kind, j, cr)]

        if way < 4:
            S["%sp%d" % (kind, j)] = over_x
        if way == 1:
            S["%spf%d" % (kind, j)] = lambda: forward(key, ref.at[j], G)
        if way > 1:
            S[name % (kind, "q", j)] = opposite
        if way == 4:
            S[name % (kind, "n", j)] = neighbours

        def wait():
            if way == 1:
                ends(key)
            elif way == 2:
                recv(*V[key], V["zq", kind, j])
            else:
                recv(V["z", kind, j], *V["zn", kind, j], V["zq", kind, j])

        return wait

    ocps = []

    def out_copy(key, j, k):
        if key == "o":
            return pltpu.make_async_copy(
                go2.at[j, 0], gout_out.at[0, pl.ds(j * 128, 128)], osem.at[0, j, 0]
            )
        return pltpu.make_async_copy(
            gi2.at[j, 0, :, pl.ds(k * 128, 128)],
            gin_out.at[0, :, pl.ds(k * 384 + j * 128, 128)],
            osem.at[1, j, k],
        )

    def gradient_steps(key, j, wait, split):
        part, b1, b2, size = (
            (pgo.at[j % 2], go1.at[j], go2.at[j], 128)
            if key == "o"
            else (pgi.at[j % 2], gi1.at[j], gi2.at[j], FB)
        )
        pieces = (("a", 0), ("b", 1)) if split else (("", 0),)
        ps = size // len(pieces)
        h = ps // 2

        def block(b):
            if key == "o":
                at = rows(b * size, size, 128)
                part[at] = lax.dot_general(
                    ag[j, :, at], cg[...].reshape(2 * G, W), FIRST, preferred_element_type=F32
                ).astype(BF16)
            else:
                at = rows(b * size, size)
                part[at] = jnp.dot(ngt[at], dg[j], preferred_element_type=F32).astype(BF16)

        def compute():
            if key == "o":
                ends(("a", j))
                ag[j, 0:G] = ab[j, :, rows(zh * 512, 512, 128)]
                whole("cp")
            else:
                ends(("d", j))
            wait()
            if j >= 2:
                drain(V["y", key, j - 2])
            block(yq)
            V["y", key, j] = []
            for name, p in pieces:
                new = [
                    rc(part.at[rows(yq * size + p * ps, h)], b1.at[rows(2 * p * h, h)], YR),
                    rc(part.at[rows(yq * size + p * ps + h, h)], b1.at[rows(2 * p * h + h, h)], YL),
                ]
                V["y1", key, j, name] = new
                V["y", key, j] += new

            @pl.loop(1, 4)
            def _(i):
                block(lax.rem(yq + i, 4))

        S["g%s%d" % (key, j)] = compute

        def piece_steps(name, p):
            def on():
                one, other = V["y1", key, j, name]
                recv(one)
                add(part.at[rows(yr * size + p * ps, h)], b1.at[rows(2 * p * h, h)])
                new = [rc(part.at[rows(yr * size + p * ps, ps)], b2.at[0, rows(p * ps, ps)], YR)]
                recv(other)
                add(part.at[rows(yl * size + p * ps + h, h)], b1.at[rows(2 * p * h + h, h)])
                new.append(rc(part.at[rows(yl * size + p * ps, ps)], b2.at[1, rows(p * ps, ps)], YL))
                V["y2", key, j, name] = new
                V["y", key, j] += new

            def end():
                recv(*V["y2", key, j, name])
                at = rows(p * ps, ps)
                b2[0, at] = (
                    part[rows(y * size + p * ps, ps)].astype(F32)
                    + b2[0, at].astype(F32)
                    + b2[1, at].astype(F32)
                ).astype(BF16)
                if name != "a":
                    for k in range(1 if key == "o" else 8):
                        cp = out_copy(key, j, k)
                        cp.start()
                        ocps.append(cp)

            S["gs%s%d%s" % (key, j, name)] = on
            S["ge%s%d%s" % (key, j, name)] = end

        for name, p in pieces:
            piece_steps(name, p)

    def chunk_steps(j):
        for kind, name, k, split in (
            (0, "dact", "d", j in SPLIT_DACT),
            (1, "pre", "p", j in SPLIT_PRE),
        ):
            for h, tail in ((0, "a"), (1, "b")) if split else ((None, ""),):
                S["%s%d%s" % (name, j, tail)] = lambda kind=kind, h=h: product(kind, j, h)
                S["rs%s%d%s" % (k, j, tail)] = lambda kind=kind, h=h: second(kind, j, h)
        S["act%d" % j] = lambda: activate(j)
        S["sd%d" % j] = lambda: both_ways(("d", j), dg.at[j], 0)
        S["af%d" % j] = lambda: forward(("a", j), ab.at[j], 0)
        S["df%d" % j] = lambda: forward(("d", j), dg.at[j], 0)
        wait_a = partner_steps("a", j, ACT_WAY[j])
        wait_d = partner_steps("d", j, DPRE_WAY[j])
        gradient_steps("o", j, wait_a, j in SPLIT_OUT)
        gradient_steps("i", j, wait_d, j in SPLIT_IN)

    for j in range(NC):
        chunk_steps(j)

    def out():
        for j in range(NC):
            ends(("a", j))

        @pl.loop(0, W // 256)
        def _(n):
            at = rows(n * 256, 256, 256)
            total = jnp.dot(ab[0], wout[0, :, at], preferred_element_type=F32)
            for j in range(1, NC):
                total += jnp.dot(ab[j], wout[j, :, at], preferred_element_type=F32)
            po[0, :, :, :, at] = total.astype(BF16).reshape(4, 2, HALF, 256)

        V["lo1"] = rc(po.at[0, 2:4], ro1.at[0], CO)

    def dna():
        for j in (0, 1):
            ends(("d", j))

        @pl.loop(0, W // 256)
        def _(n):
            at = rows(n * 256, 256, 256)
            acc[:, at] = sum(
                lax.dot_general(dg[j, 0:G], win[j, at], LAST, preferred_element_type=F32)
                for j in (0, 1)
            )

    def dnb():
        ends(("d", 2))

        @pl.loop(0, W // 256)
        def _(n):
            at = rows(n * 256, 256, 256)
            total = acc[:, at] + lax.dot_general(
                dg[2, 0:G], win[2, at], LAST, preferred_element_type=F32
            )
            po[1, :, :, :, at] = total.astype(BF16).reshape(4, 2, HALF, 256)

        V["dn1"] = rc(po.at[1, 2:4], ro1.at[1], CO)

    def row_second(q, key):
        recv(V[key])
        add(po.at[q, 0:2, 1], ro1.at[q, :, 1])
        return rc(po.at[q, 0:2, 1], ro2.at[q], ZL)

    def row_sum(q):
        return (
            po[q, 0:2, 0].astype(F32) + ro1[q, :, 0].astype(F32) + ro2[q].astype(F32)
        ).reshape(T, W)

    def lo2():
        V["lo2"] = row_second(0, "lo1")

    def dn2():
        V["dn2"] = row_second(1, "dn1")

    def lo3():
        recv(V["lo2"])
        layer_out[...] = (tok[...].astype(F32) + row_sum(0)).astype(BF16)

    def fin():
        recv(V["dn2"])
        mean, inverse = mean_inverse()
        dnorm = row_sum(1)
        xhat = (tok[...].astype(F32) - mean) * inverse
        gains[0] = jnp.sum((dnorm * xhat).reshape(T // 8, 8, W), axis=0)
        V["ga"] = rc(gains.at[0], gains.at[1], CO)
        dxhat = dnorm * gain[...]
        tails[0] = two(
            jnp.sum(dxhat, axis=1, keepdims=True), jnp.sum(dxhat * xhat, axis=1, keepdims=True)
        )
        V["ta"] = rc(tails.at[0], tails.at[1], XA)

    def t2():
        recv(V["ta"])
        tails[2] = tails[0] + tails[1]
        V["tb"] = rc(tails.at[2], tails.at[3], XB)

    def t3():
        recv(V["tb"])
        tails[4] = tails[2] + tails[3]
        mean, inverse = mean_inverse()
        first = tails[4, :, 0:1] / MODEL_WIDTH
        second = tails[4, :, 1:2] / MODEL_WIDTH
        xhat = (tok[...].astype(F32) - mean) * inverse
        token_grad[...] = (
            cot[...].astype(F32) + inverse * (row_sum(1) * gain[...] - first - xhat * second)
        ).astype(BF16)

    def gain_step(i, old, new, dev):
        def step():
            recv(V[old])
            gains[2 * i + 2] = gains[2 * i] + gains[2 * i + 1]
            V[new] = rc(gains.at[2 * i + 2], gains.at[2 * i + 3], dev)

        return step

    def gz():
        recv(V["ge"])
        gain_grad[...] = jnp.sum(gains[8] + gains[9], axis=0, keepdims=True)

    S.update(out=out, dna=dna, dnb=dnb, lo2=lo2, dn2=dn2, lo3=lo3, fin=fin, t2=t2, t3=t3, gz=gz)
    S["gb"] = gain_step(0, "ga", "gb", ZL)
    S["gc"] = gain_step(1, "gb", "gc", ZH)
    S["gd"] = gain_step(2, "gc", "gd", YA)
    S["ge"] = gain_step(3, "gd", "ge", YB)

    assert sorted(S) == sorted(ORDER)
    for name in ORDER:
        S[name]()
    drain(list(sends))
    for cp in ocps:
        cp.wait()
    assert count[0] <= N_COPIES, count[0]


N_COPIES = 180


def body(tokens, norm_scale_gain, in_weight, out_weight, cotangent):
    vm = pl.BlockSpec(memory_space=pltpu.VMEM)
    hbm = pl.BlockSpec(memory_space=pl.ANY)
    layer_out, token_grad, gain_grad, grad_in, grad_out = pl.pallas_call(
        kernel,
        out_shape=(
            jax.ShapeDtypeStruct((T, W), BF16),
            jax.ShapeDtypeStruct((T, W), BF16),
            jax.ShapeDtypeStruct((1, W), F32),
            jax.ShapeDtypeStruct((1, FB, NC * H), BF16),
            jax.ShapeDtypeStruct((1, NC * 128, W), BF16),
        ),
        in_specs=[vm, vm, hbm, hbm, vm],
        out_specs=(vm, vm, vm, hbm, hbm),
        scratch_shapes=[
            pltpu.VMEM((NC, W, H), BF16),
            pltpu.VMEM((NC, H, W), BF16),
            pltpu.VMEM((4, 2, HALF, W), BF16),
            pltpu.VMEM((4, 2, HALF, FG), BF16),
            pltpu.VMEM((FG, 2 * G), BF16),
            pltpu.VMEM((8, 2, HALF, W), BF16),
            pltpu.VMEM((NC, G, H), BF16),
            pltpu.VMEM((NC, 2 * G, 512), BF16),
            pltpu.VMEM((NC, 2 * G, H), BF16),
            pltpu.VMEM((2, 2, 4, 2, HALF, H), BF16),
            pltpu.VMEM((2, NC, 2, HALF, H), BF16),
            pltpu.VMEM((2, NC, 2, 2, HALF, H), BF16),
            pltpu.VMEM((2, 4, 2, HALF, W), BF16),
            pltpu.VMEM((2, 2, 2, HALF, W), BF16),
            pltpu.VMEM((2, 2, HALF, W), BF16),
            pltpu.VMEM((G, W), F32),
            pltpu.VMEM((2, FG, H), BF16),
            pltpu.VMEM((2, 512, W), BF16),
            pltpu.VMEM((NC, FB, H), BF16),
            pltpu.VMEM((NC, 2, FB, H), BF16),
            pltpu.VMEM((NC, 128, W), BF16),
            pltpu.VMEM((NC, 2, 128, W), BF16),
            pltpu.VMEM((5, T, 128), F32),
            pltpu.VMEM((5, T, 128), F32),
            pltpu.VMEM((10, 8, W), F32),
            pltpu.SemaphoreType.DMA((NC, 8)),
            pltpu.SemaphoreType.DMA((NC, 8)),
            pltpu.SemaphoreType.DMA((2, NC, 8)),
            pltpu.SemaphoreType.DMA((N_COPIES,)),
            pltpu.SemaphoreType.DMA((N_COPIES,)),
        ],
        compiler_params=pltpu.CompilerParams(
            collective_id=0, has_side_effects=True, vmem_limit_bytes=63 * 2**20
        ),
        cost_estimate=pl.CostEstimate(
            flops=22 * 10**9, bytes_accessed=24 * 10**6, transcendentals=600000
        ),
        name="feed_forward",
    )(tokens, norm_scale_gain.reshape(1, W), in_weight, out_weight, cotangent)
    return (layer_out, token_grad, gain_grad.reshape(W), grad_in, grad_out)


def solution(mesh):
    in_specs = (
        P(("dp", "row"), "col"),
        P("col"),
        P("col", "row"),
        P("row", "col"),
        P(("dp", "row"), "col"),
    )
    out_specs = (
        P(("dp", "row"), "col"),
        P(("dp", "row"), "col"),
        P("col"),
        P("dp", "col", "row"),
        P("dp", "row", "col"),
    )
    return jax.shard_map(body, mesh=mesh, in_specs=in_specs, out_specs=out_specs, check_vma=False)
```

```python
import jax
import jax.numpy as jnp
from jax import lax
from jax.experimental import pallas as pl
from jax.experimental.pallas import tpu as pltpu
from jax.sharding import PartitionSpec as P

MODEL_WIDTH = 6144
EPS = 1e-06
MESH = pl.DeviceIdType.MESH
F32 = jnp.float32
BF16 = jnp.bfloat16

T = 96
G = 384
W = 1536
H = 1024
NC = 3
HALF = T // 2
FB = 192
FG = 4 * FB
LAST = (((1,), (1,)), ((), ()))
FIRST = (((0,), (0,)), ((), ()))

ACT_WAY = (2, 2, 2)
DPRE_WAY = (4, 2, 2)
SPLIT_DACT = (0, 1)
SPLIT_PRE = (0,)
SPLIT_IN = (0, 2)
SPLIT_OUT = (2,)
SPLIT_ACT = (0,)

ORDER = (
    "cotz", "cotc", "st1", "dact0a", "dact1a", "st3", "rsd0a", "coth", "rsd1a", "cotf", "pre0a",
    "norh", "dact1b", "dact0b", "rsp0a", "norf", "rsd0b", "pre0b", "act0a", "rsp0b", "dgr0a",
    "cph", "af0a", "act0b", "pre2", "za0", "nph", "af0b", "dgr0b", "df0a", "zaq0", "zd0", "ap0",
    "pre1", "rsp2", "cpf", "zdn0", "df0b", "go0", "npf", "rsp1", "ngt1", "gso0", "act2", "zdq0",
    "ngt0", "za2", "act1", "af2", "gi0", "af1", "gsi0a", "ap2", "geo0", "za1", "dact2", "zaq2",
    "zaq1", "gsi0b", "rsd1b", "ap1", "gei0a", "rsd2", "go2", "dgr1", "go1", "gso2b", "zd1",
    "gso2a", "dgr2", "out", "df1", "zd2", "gso1", "df2", "gei0b", "zdq1", "dp1", "dna", "zdq2",
    "dp2", "dnb", "gi1", "dn2", "geo2b", "gi2", "gsi2a", "geo1", "fin", "gsi1", "gb", "gc",
    "gei2a", "lo2", "gd", "geo2a", "gsi2b", "gei1", "ge", "t3", "lo3", "gei2b", "gz",
)


def rows(start, size, unit=16):
    return pl.ds(pl.multiple_of(start, unit), size)


def kernel(
    tok, gain, win_hbm, wout_hbm, cot,
    layer_out, token_grad, gain_grad, gin_out, gout_out,
    win, wout, nf, ngp, ngt, cg, ab, ag, dg, px, rx1, rx2, po, ro1, ro2, acc, slope,
    pgi, pgo, gi1, gi2, go1, go2, stat, tails, gains, wsem_in, wsem_out, osem, ssem, rsem,
):
    d, r, c = lax.axis_index("dp"), lax.axis_index("row"), lax.axis_index("col")
    zh, y = lax.div(d, 4), lax.rem(d, 4)
    zl, co = lax.div(r, 2), lax.rem(r, 2)
    cr, cl = lax.rem(c + 1, 4), lax.rem(c + 3, 4)
    yr, yl = lax.rem(y + 1, 4), lax.rem(y + 3, 4)
    cq, yq = lax.rem(c + 2, 4), lax.rem(y + 2, 4)
    XR, XL, XQ = (d, r, cr), (d, r, cl), (d, r, cq)
    YR, YL = (zh * 4 + yr, r, c), (zh * 4 + yl, r, c)
    ZL, ZH = (d, (1 - zl) * 2 + co, c), ((1 - zh) * 4 + y, r, c)
    CO = (d, zl * 2 + 1 - co, c)
    YA = (zh * 4 + y + 1 - 2 * lax.rem(y, 2), r, c)
    YB = (zh * 4 + 3 - y, r, c)

    def slot(ref, i, first=0):
        return ref.at[pl.ds(first + 2 * (i % 2), 2), i // 2]

    count = [0]
    sends = []
    V = {"cot": {}}

    def rc(src, dst, dev):
        i = count[0]
        count[0] += 1
        cp = pltpu.make_async_remote_copy(
            src, dst, ssem.at[i], rsem.at[i], device_id=dev, device_id_type=MESH
        )
        cp.start()
        sends.append(cp)
        return cp

    def recv(*cps):
        for cp in cps:
            cp.wait_recv()

    def drain(cps):
        for cp in cps:
            cp.wait_send()
        gone = [id(cp) for cp in cps]
        sends[:] = [cp for cp in sends if id(cp) not in gone]

    def win_copy(j, k):
        return pltpu.make_async_copy(
            win_hbm.at[:, rows(k * 384 + j * 128, 128, 128)],
            win.at[j, :, rows(k * 128, 128, 128)],
            wsem_in.at[j, k],
        )

    def wout_copy(j, k):
        return pltpu.make_async_copy(
            wout_hbm.at[rows(k * 384 + j * 128, 128, 128)],
            wout.at[j, rows(k * 128, 128, 128)],
            wsem_out.at[j, k],
        )

    for j in range(NC):

        @pl.loop(0, 8)
        def _(k):
            wout_copy(j, k).start()
            win_copy(j, k).start()

    loaded = []

    def need(copy, key, j):
        if (key, j) not in loaded:
            loaded.append((key, j))

            @pl.loop(0, 8)
            def _(k):
                copy(j, k).wait()

    barrier = pltpu.get_barrier_semaphore()
    for dev in (XR, XL, XQ, YR, YL, ZL, ZH, CO):
        pl.semaphore_signal(barrier, inc=1, device_id=dev, device_id_type=MESH)

    cg[0:2, 0] = cot[...].reshape(2, HALF, W)
    x = tok[...].astype(F32)
    lane = lax.broadcasted_iota(jnp.int32, (T, 128), 1)

    def two(a, b):
        return jnp.where(lane == 0, a, jnp.where(lane == 1, b, 0.0))

    stat[0] = two(jnp.sum(x, axis=1, keepdims=True), jnp.sum(x * x, axis=1, keepdims=True))
    pl.semaphore_wait(barrier, 8)

    def mean_inverse():
        mean = stat[4, :, 0:1] / MODEL_WIDTH
        return mean, lax.rsqrt(stat[4, :, 1:2] / MODEL_WIDTH - mean * mean + EPS)

    S = {}

    def spread(key, ref, first=0):
        own = slot(ref, 0, first)
        V[key] = {0: rc(own, slot(ref, 1, first), CO), 1: rc(own, slot(ref, 2, first), ZL)}

    def spread_on(key, ref, first=0):
        recv(V[key][1])
        V[key][2] = rc(slot(ref, 2, first), slot(ref, 3, first), CO)

    done = []

    def once(key, *cps):
        if key not in done:
            done.append(key)
            recv(*cps)

    def own_chip(key):
        once(key + "0", V[key][0])

    def whole(key):
        own_chip(key)
        once(key + "1", V[key][2])

    def cotc():
        V["cot"][0] = rc(slot(cg, 0), slot(cg, 1), CO)

    def cotz():
        V["cot"][1] = rc(slot(cg, 0), slot(cg, 2), ZL)

    S["cotc"], S["cotz"] = cotc, cotz
    S["cotf"] = lambda: spread_on("cot", cg)

    def to_column(key, ref):
        V[key] = [rc(ref.at[0], ref.at[1 + i], dev) for i, dev in enumerate((XR, XL, XQ))]

    def of_column(key, ref):
        recv(*V[key])
        ref[4] = (ref[0] + ref[3]) + (ref[1] + ref[2])

    def st1():
        to_column("sa", stat)

    def st3():
        of_column("sa", stat)
        mean, inverse = mean_inverse()
        normed = ((tok[...].astype(F32) - mean) * inverse * gain[...].reshape(1, W)).astype(BF16)
        nf[0:2, 0] = normed.reshape(2, HALF, W)
        spread("nor", nf)

    S["st1"], S["st3"] = st1, st3
    S["norf"] = lambda: spread_on("nor", nf)

    def coth():
        V["coth"] = rc(slot(cg, 0), slot(cg, 0, 4), ZH)

    def norh():
        V["norh"] = rc(
            nf.at[0:2, 0, :, rows((1 - zh) * FG, FG, 128)], slot(ngp, 0), ZH
        )

    def cph():
        recv(V["coth"])
        spread("cp", cg, 4)

    def nph():
        recv(V["norh"])
        spread("np", ngp)

    def ngt0():
        whole("nor")
        ngt[:, 0:G] = jnp.transpose(nf[:, :, :, rows(zh * FG, FG, 128)].reshape(G, FG))

    def ngt1():
        whole("np")
        ngt[:, G:] = jnp.transpose(ngp[...].reshape(G, FG))

    S["coth"], S["norh"], S["cph"], S["nph"] = coth, norh, cph, nph
    S["ngt0"], S["ngt1"] = ngt0, ngt1
    S["cpf"] = lambda: spread_on("cp", cg, 4)
    S["npf"] = lambda: spread_on("np", ngp)

    def add(part, buf):
        part[...] = (part[...].astype(F32) + buf[...].astype(F32)).astype(BF16)

    CA, CB = pl.ds(0, H // 2), pl.ds(H // 2, H // 2)

    def product(kind, j, h):
        key = "cot" if kind == 0 else "nor"
        (need(wout_copy, "o", j) if kind == 0 else need(win_copy, "i", j))
        own_chip(key) if h == 0 else whole(key)
        if j >= 2 and h != 1:
            drain(V["x1", kind, j - 2] + V["x2", kind, j - 2])
        src = cg if kind == 0 else nf
        part = px.at[kind, j % 2]

        @pl.loop(0, H // 256)
        def _(n):
            at = rows(n * 256, 256, 256)
            if h is None:
                left = src[0:4].reshape(G, W)
            else:
                left = src[0:4, h].reshape(G // 2, W)
            if kind == 0:
                out = lax.dot_general(left, wout[j, at], LAST, preferred_element_type=F32)
            else:
                out = jnp.dot(left, win[j, :, at], preferred_element_type=F32)
            if h is None:
                part[:, :, :, at] = out.astype(BF16).reshape(4, 2, HALF, 256)
            else:
                part[:, h, :, at] = out.astype(BF16).reshape(4, HALF, 256)

        buf = rx1.at[kind, j]
        if h is None:
            new = [rc(part.at[cq, 0], buf.at[0], XR), rc(part.at[cq, 1], buf.at[1], XL)]
        else:
            new = [
                rc(part.at[cq, h, :, CA], buf.at[h, :, CA], XR),
                rc(part.at[cq, h, :, CB], buf.at[h, :, CB], XL),
            ]
        V["x1", kind, j, h] = new
        V["x1", kind, j] = V.get(("x1", kind, j), []) + new

    def second(kind, j, h):
        one, other = V["x1", kind, j, h]
        part, buf, out = px.at[kind, j % 2], rx1.at[kind, j], rx2.at[kind, j]
        new = []
        if h is None:
            recv(one)
            add(part.at[cr, 0], buf.at[0])
            new.append(rc(part.at[cr], out.at[0], XR))
            recv(other)
            add(part.at[cl, 1], buf.at[1])
            new.append(rc(part.at[cl], out.at[1], XL))
        else:
            recv(one)
            add(part.at[cr, h, :, CA], buf.at[h, :, CA])
            new.append(rc(part.at[cr, h], out.at[0, h], XR))
            recv(other)
            add(part.at[cl, h, :, CB], buf.at[h, :, CB])
            new.append(rc(part.at[cl, h], out.at[1, h], XL))
        V["x2", kind, j, h] = new
        V["x2", kind, j] = V.get(("x2", kind, j), []) + new

    def total(kind, j, h, at):
        here = slice(None) if h is None else h
        return (
            px[kind, j % 2, c, here, :, at].astype(F32)
            + rx2[kind, j, 0, here, :, at].astype(F32)
            + rx2[kind, j, 1, here, :, at].astype(F32)
        ).reshape(T if h is None else HALF, 256)

    def arrived(kind, j, h):
        split = j in (SPLIT_DACT, SPLIT_PRE)[kind]
        for part in ((0, 1) if h is None else (h,)) if split else (None,):
            once(("x2", kind, j, part), *V["x2", kind, j, part])

    def own_rows(h):
        return rows(c * T, T) if h is None else rows(c * T + h * HALF, HALF)

    def activate(j, h):
        arrived(1, j, h)
        to = slice(0, T) if h is None else slice(h * HALF, (h + 1) * HALF)

        @pl.loop(0, H // 256)
        def _(n):
            at = rows(n * 256, 256, 256)
            pre = total(1, j, h, at)
            cdf = 0.5 * (1.0 + lax.erf(pre * 0.7071067811865476))
            dens = jnp.exp(-0.5 * pre * pre) * 0.3989422804014327
            ab[j, own_rows(h), at] = (pre * cdf).astype(BF16)
            slope[j % 2, to, at] = cdf + pre * dens

        both_ways(("a", j, h), ab.at[j], 0, h)

    def dgelu(j, h):
        arrived(0, j, h)
        to = slice(0, T) if h is None else slice(h * HALF, (h + 1) * HALF)

        @pl.loop(0, H // 256)
        def _(n):
            at = rows(n * 256, 256, 256)
            dg[j, own_rows(h), at] = (total(0, j, h, at) * slope[j % 2, to, at]).astype(BF16)

        both_ways(("d", j, h), dg.at[j], 0, h)

    def both_ways(key, ref, base, h=None):
        own = ref.at[rows(base + c * T, T) if h is None else rows(base + c * T + h * HALF, HALF)]
        V[key] = [rc(own, own, XR), rc(own, own, XL)]

    def forward(key, ref, base, h=None):
        one, other = V[key]
        once((key, 0), one)
        if h is None:
            a = ref.at[rows(base + cl * T, HALF)]
            b = ref.at[rows(base + cr * T + HALF, HALF)]
        else:
            a = ref.at[rows(base + cl * T + h * HALF, HALF), CA]
            b = ref.at[rows(base + cr * T + h * HALF, HALF), CB]
        V[key].append(rc(a, a, XR))
        once((key, 1), other)
        V[key].append(rc(b, b, XL))

    def ends(key):
        once((key, 2), V[key][2])
        once((key, 3), V[key][3])

    def halves(j):
        return ((0, "a"), (1, "b")) if j in SPLIT_ACT else ((None, ""),)

    def all_ends(kind, j):
        for h, _ in halves(j):
            ends((kind, j, h))

    def over_z(kind, j, piece):
        if kind == "a":
            return rc(
                ab.at[j, rows(piece * T, T), rows((1 - zh) * 512, 512, 128)],
                ag.at[j, rows(G + piece * T, T)],
                ZH,
            )
        return rc(dg.at[j, rows(piece * T, T)], dg.at[j, rows(G + piece * T, T)], ZH)

    def partner_steps(kind, j, way):
        ref = ag if kind == "a" else dg
        key = (kind + "p", j)
        name = "z%s%s%d"

        def z_own():
            V["z", kind, j] = over_z(kind, j, c)

        S["z%s%d" % (kind, j)] = z_own

        def over_x():
            once(("z", kind, j), V["z", kind, j])
            both_ways(key, ref.at[j], G)

        def opposite():
            all_ends(kind, j)
            V["zq", kind, j] = over_z(kind, j, cq)

        def neighbours():
            for h, _ in halves(j):
                for i in (0, 1):
                    once(((kind, j, h), i), V[kind, j, h][i])
            V["zn", kind, j] = [over_z(kind, j, cl), over_z(kind, j, cr)]

        if way < 4:
            S["%sp%d" % (kind, j)] = over_x
        if way == 1:
            S["%spf%d" % (kind, j)] = lambda: forward(key, ref.at[j], G)
        if way > 1:
            S[name % (kind, "q", j)] = opposite
        if way == 4:
            S[name % (kind, "n", j)] = neighbours

        def wait():
            if way == 1:
                ends(key)
            elif way == 2:
                recv(*V[key], V["zq", kind, j])
            else:
                recv(V["z", kind, j], *V["zn", kind, j], V["zq", kind, j])

        return wait

    ocps = []

    def out_copy(key, j, k):
        if key == "o":
            return pltpu.make_async_copy(
                go2.at[j, 0], gout_out.at[0, pl.ds(j * 128, 128)], osem.at[0, j, 0]
            )
        return pltpu.make_async_copy(
            gi2.at[j, 0, :, pl.ds(k * 128, 128)],
            gin_out.at[0, :, pl.ds(k * 384 + j * 128, 128)],
            osem.at[1, j, k],
        )

    def gradient_steps(key, j, wait, split):
        part, b1, b2, size = (
            (pgo.at[j % 2], go1.at[j], go2.at[j], 128)
            if key == "o"
            else (pgi.at[j % 2], gi1.at[j], gi2.at[j], FB)
        )
        pieces = (("a", 0), ("b", 1)) if split else (("", 0),)
        ps = size // len(pieces)
        h = ps // 2

        def block(b):
            if key == "o":
                at = rows(b * size, size, 128)
                part[at] = lax.dot_general(
                    ag[j, :, at], cg[...].reshape(2 * G, W), FIRST, preferred_element_type=F32
                ).astype(BF16)
            else:
                at = rows(b * size, size)
                part[at] = jnp.dot(ngt[at], dg[j], preferred_element_type=F32).astype(BF16)

        def compute():
            if key == "o":
                all_ends("a", j)
                ag[j, 0:G] = ab[j, :, rows(zh * 512, 512, 128)]
                whole("cp")
            else:
                all_ends("d", j)
            wait()
            if j >= 2:
                drain(V["y", key, j - 2])
            block(yq)
            V["y", key, j] = []
            for name, p in pieces:
                new = [
                    rc(part.at[rows(yq * size + p * ps, h)], b1.at[rows(2 * p * h, h)], YR),
                    rc(part.at[rows(yq * size + p * ps + h, h)], b1.at[rows(2 * p * h + h, h)], YL),
                ]
                V["y1", key, j, name] = new
                V["y", key, j] += new

            @pl.loop(1, 4)
            def _(i):
                block(lax.rem(yq + i, 4))

        S["g%s%d" % (key, j)] = compute

        def piece_steps(name, p):
            def on():
                one, other = V["y1", key, j, name]
                recv(one)
                add(part.at[rows(yr * size + p * ps, h)], b1.at[rows(2 * p * h, h)])
                new = [rc(part.at[rows(yr * size + p * ps, ps)], b2.at[0, rows(p * ps, ps)], YR)]
                recv(other)
                add(part.at[rows(yl * size + p * ps + h, h)], b1.at[rows(2 * p * h + h, h)])
                new.append(rc(part.at[rows(yl * size + p * ps, ps)], b2.at[1, rows(p * ps, ps)], YL))
                V["y2", key, j, name] = new
                V["y", key, j] += new

            def end():
                recv(*V["y2", key, j, name])
                at = rows(p * ps, ps)
                b2[0, at] = (
                    part[rows(y * size + p * ps, ps)].astype(F32)
                    + b2[0, at].astype(F32)
                    + b2[1, at].astype(F32)
                ).astype(BF16)
                V["left", key, j] = V.get(("left", key, j), len(pieces)) - 1
                if V["left", key, j] == 0:
                    for k in range(1 if key == "o" else 8):
                        cp = out_copy(key, j, k)
                        cp.start()
                        ocps.append(cp)

            S["gs%s%d%s" % (key, j, name)] = on
            S["ge%s%d%s" % (key, j, name)] = end

        for name, p in pieces:
            piece_steps(name, p)

    def chunk_steps(j):
        for kind, name, k, split in (
            (0, "dact", "d", j in SPLIT_DACT),
            (1, "pre", "p", j in SPLIT_PRE),
        ):
            for h, tail in ((0, "a"), (1, "b")) if split else ((None, ""),):
                S["%s%d%s" % (name, j, tail)] = lambda kind=kind, h=h: product(kind, j, h)
                S["rs%s%d%s" % (k, j, tail)] = lambda kind=kind, h=h: second(kind, j, h)
        for h, tail in halves(j):
            S["act%d%s" % (j, tail)] = lambda h=h: activate(j, h)
            S["dgr%d%s" % (j, tail)] = lambda h=h: dgelu(j, h)
            S["af%d%s" % (j, tail)] = lambda h=h: forward(("a", j, h), ab.at[j], 0, h)
            S["df%d%s" % (j, tail)] = lambda h=h: forward(("d", j, h), dg.at[j], 0, h)
        wait_a = partner_steps("a", j, ACT_WAY[j])
        wait_d = partner_steps("d", j, DPRE_WAY[j])
        gradient_steps("o", j, wait_a, j in SPLIT_OUT)
        gradient_steps("i", j, wait_d, j in SPLIT_IN)

    for j in range(NC):
        chunk_steps(j)

    def out():
        for j in range(NC):
            all_ends("a", j)

        @pl.loop(0, W // 256)
        def _(n):
            at = rows(n * 256, 256, 256)
            total = jnp.dot(ab[0], wout[0, :, at], preferred_element_type=F32)
            for j in range(1, NC):
                total += jnp.dot(ab[j], wout[j, :, at], preferred_element_type=F32)
            po[0, :, :, :, at] = total.astype(BF16).reshape(4, 2, HALF, 256)

        V["lo1"] = rc(po.at[0, 2:4], ro1.at[0], CO)

    def dna():
        for j in (0, 1):
            all_ends("d", j)

        @pl.loop(0, W // 256)
        def _(n):
            at = rows(n * 256, 256, 256)
            acc[:, at] = sum(
                lax.dot_general(dg[j, 0:G], win[j, at], LAST, preferred_element_type=F32)
                for j in (0, 1)
            )

    def dnb():
        all_ends("d", 2)

        @pl.loop(0, W // 256)
        def _(n):
            at = rows(n * 256, 256, 256)
            total = acc[:, at] + lax.dot_general(
                dg[2, 0:G], win[2, at], LAST, preferred_element_type=F32
            )
            po[1, :, :, :, at] = total.astype(BF16).reshape(4, 2, HALF, 256)

        V["dn1"] = rc(po.at[1, 2:4], ro1.at[1], CO)

    def row_second(q, key):
        recv(V[key])
        add(po.at[q, 0:2, 1], ro1.at[q, :, 1])
        return rc(po.at[q, 0:2, 1], ro2.at[q], ZL)

    def row_sum(q):
        return (
            po[q, 0:2, 0].astype(F32) + ro1[q, :, 0].astype(F32) + ro2[q].astype(F32)
        ).reshape(T, W)

    def lo2():
        V["lo2"] = row_second(0, "lo1")

    def dn2():
        V["dn2"] = row_second(1, "dn1")

    def lo3():
        recv(V["lo2"])
        layer_out[...] = (tok[...].astype(F32) + row_sum(0)).astype(BF16)

    def fin():
        recv(V["dn2"])
        mean, inverse = mean_inverse()
        dnorm = row_sum(1)
        xhat = (tok[...].astype(F32) - mean) * inverse
        gains[0] = jnp.sum((dnorm * xhat).reshape(T // 8, 8, W), axis=0)
        V["ga"] = rc(gains.at[0], gains.at[1], CO)
        dxhat = dnorm * gain[...].reshape(1, W)
        tails[0] = two(
            jnp.sum(dxhat, axis=1, keepdims=True), jnp.sum(dxhat * xhat, axis=1, keepdims=True)
        )
        to_column("ta", tails)

    def t3():
        of_column("ta", tails)
        mean, inverse = mean_inverse()
        first = tails[4, :, 0:1] / MODEL_WIDTH
        second = tails[4, :, 1:2] / MODEL_WIDTH
        xhat = (tok[...].astype(F32) - mean) * inverse
        token_grad[...] = (
            cot[...].astype(F32) + inverse * (row_sum(1) * gain[...].reshape(1, W) - first - xhat * second)
        ).astype(BF16)

    def gain_step(i, old, new, dev):
        def step():
            recv(V[old])
            gains[2 * i + 2] = gains[2 * i] + gains[2 * i + 1]
            V[new] = rc(gains.at[2 * i + 2], gains.at[2 * i + 3], dev)

        return step

    def gz():
        recv(V["ge"])
        gain_grad[...] = jnp.sum(gains[8] + gains[9], axis=0)

    S.update(out=out, dna=dna, dnb=dnb, lo2=lo2, dn2=dn2, lo3=lo3, fin=fin, t3=t3, gz=gz)
    S["gb"] = gain_step(0, "ga", "gb", ZL)
    S["gc"] = gain_step(1, "gb", "gc", ZH)
    S["gd"] = gain_step(2, "gc", "gd", YA)
    S["ge"] = gain_step(3, "gd", "ge", YB)

    assert sorted(S) == sorted(ORDER)
    for name in ORDER:
        S[name]()
    drain(list(sends))
    for cp in ocps:
        cp.wait()
    assert count[0] <= N_COPIES, count[0]


N_COPIES = 230


def copy_kernel(*refs):
    src, dst, via, (one, two) = refs[:5], refs[5:10], refs[10:15], refs[15:]
    first = [pltpu.make_async_copy(src[i], via[i], one.at[i]) for i in range(5)]
    then = [pltpu.make_async_copy(via[i], dst[i], two.at[i]) for i in range(5)]
    for cp in first:
        cp.start()
    for a, b in zip(first, then):
        a.wait()
        b.start()
    for cp in then:
        cp.wait()


def body(tokens, norm_scale_gain, in_weight, out_weight, cotangent):
    vm = pl.BlockSpec(memory_space=pltpu.VMEM)
    hbm = pl.BlockSpec(memory_space=pl.ANY)
    layer_out, token_grad, gain_grad, grad_in, grad_out = pl.pallas_call(
        kernel,
        out_shape=(
            jax.ShapeDtypeStruct((T, W), BF16),
            jax.ShapeDtypeStruct((T, W), BF16),
            jax.ShapeDtypeStruct((W,), F32),
            jax.ShapeDtypeStruct((1, FB, NC * H), BF16),
            jax.ShapeDtypeStruct((1, NC * 128, W), BF16),
        ),
        in_specs=[vm, vm, hbm, hbm, vm],
        out_specs=(vm, vm, vm, hbm, hbm),
        scratch_shapes=[
            pltpu.VMEM((NC, W, H), BF16),
            pltpu.VMEM((NC, H, W), BF16),
            pltpu.VMEM((4, 2, HALF, W), BF16),
            pltpu.VMEM((4, 2, HALF, FG), BF16),
            pltpu.VMEM((FG, 2 * G), BF16),
            pltpu.VMEM((8, 2, HALF, W), BF16),
            pltpu.VMEM((NC, G, H), BF16),
            pltpu.VMEM((NC, 2 * G, 512), BF16),
            pltpu.VMEM((NC, 2 * G, H), BF16),
            pltpu.VMEM((2, 2, 4, 2, HALF, H), BF16),
            pltpu.VMEM((2, NC, 2, HALF, H), BF16),
            pltpu.VMEM((2, NC, 2, 2, HALF, H), BF16),
            pltpu.VMEM((2, 4, 2, HALF, W), BF16),
            pltpu.VMEM((2, 2, 2, HALF, W), BF16),
            pltpu.VMEM((2, 2, HALF, W), BF16),
            pltpu.VMEM((G, W), F32),
            pltpu.VMEM((2, T, H), F32),
            pltpu.VMEM((2, FG, H), BF16),
            pltpu.VMEM((2, 512, W), BF16),
            pltpu.VMEM((NC, FB, H), BF16),
            pltpu.VMEM((NC, 2, FB, H), BF16),
            pltpu.VMEM((NC, 128, W), BF16),
            pltpu.VMEM((NC, 2, 128, W), BF16),
            pltpu.VMEM((5, T, 128), F32),
            pltpu.VMEM((5, T, 128), F32),
            pltpu.VMEM((10, 8, W), F32),
            pltpu.SemaphoreType.DMA((NC, 8)),
            pltpu.SemaphoreType.DMA((NC, 8)),
            pltpu.SemaphoreType.DMA((2, NC, 8)),
            pltpu.SemaphoreType.DMA((N_COPIES,)),
            pltpu.SemaphoreType.DMA((N_COPIES,)),
        ],
        compiler_params=pltpu.CompilerParams(
            collective_id=0, has_side_effects=True, vmem_limit_bytes=63 * 2**20
        ),
        cost_estimate=pl.CostEstimate(
            flops=22 * 10**9, bytes_accessed=24 * 10**6, transcendentals=600000
        ),
        name="feed_forward",
    )(tokens, norm_scale_gain, in_weight, out_weight, cotangent)
    arrays = (layer_out, token_grad, gain_grad, grad_in, grad_out)
    return pl.pallas_call(
        copy_kernel,
        out_shape=tuple(jax.ShapeDtypeStruct(a.shape, a.dtype) for a in arrays),
        in_specs=[hbm] * 5,
        out_specs=(hbm,) * 5,
        scratch_shapes=[pltpu.VMEM(a.shape, a.dtype) for a in arrays]
        + [pltpu.SemaphoreType.DMA((5,)), pltpu.SemaphoreType.DMA((5,))],
        name="results",
    )(*arrays)


def solution(mesh):
    in_specs = (
        P(("dp", "row"), "col"),
        P("col"),
        P("col", "row"),
        P("row", "col"),
        P(("dp", "row"), "col"),
    )
    out_specs = (
        P(("dp", "row"), "col"),
        P(("dp", "row"), "col"),
        P("col"),
        P("dp", "col", "row"),
        P("dp", "row", "col"),
    )
    return jax.shard_map(body, mesh=mesh, in_specs=in_specs, out_specs=out_specs, check_vma=False)
```

```python
import jax
import jax.numpy as jnp
from jax import lax
from jax.experimental import pallas as pl
from jax.experimental.pallas import tpu as pltpu
from jax.sharding import PartitionSpec as P

MODEL_WIDTH = 6144
EPS = 1e-06
MESH = pl.DeviceIdType.MESH
F32 = jnp.float32
BF16 = jnp.bfloat16

T = 96
G = 384
W = 1536
H = 1024
NC = 3
HALF = T // 2
FB = 192
FG = 4 * FB
LAST = (((1,), (1,)), ((), ()))
FIRST = (((0,), (0,)), ((), ()))

DPRE_WAY = (4, 2, 2)
SPLIT_DACT = (0, 1)
SPLIT_PRE = (0,)
SPLIT_IN = (2,)
SPLIT_ACT = (0,)

ORDER = (
    "cotc", "cotz", "st1", "dact0a", "dact1a", "rsd0a", "st3", "rsd1a", "cotf", "cyb", "pre0a",
    "dact0b", "dact1b", "norh", "cya", "rsp0a", "rsd0b", "norf", "rsd1b", "pre0b", "act0a", "pre1",
    "ngt0", "rsp0b", "af0a", "nph", "dgr0a", "act0b", "cybf", "dgr0b", "zd0", "rsp1", "cyaf",
    "pre2", "zdn0", "df0a", "af0b", "df0b", "npf", "ngt1", "act1", "ya0", "zdq0", "dgr1", "zd1",
    "cyc", "dact2", "af1", "gi0", "df1", "rsp2", "go0", "ya1", "zdq1", "rsd2", "gsi0", "act2",
    "dgr2", "zd2", "geo0", "go1", "af2", "dna", "df2", "ya2", "dp1", "zdq2", "dp2", "dnb", "dn2",
    "gi1", "gei0", "gi2", "go2", "gsi1", "fin", "gb", "gsi2b", "out", "gc", "lo2", "gd", "gsi2a",
    "ge", "geo2", "gei1", "gei2b", "t3", "lo3", "geo1", "gei2a", "gz",
)


def rows(start, size, unit=16):
    return pl.ds(pl.multiple_of(start, unit), size)


def kernel(
    tok, gain, win_hbm, wout_hbm, cot,
    layer_out, token_grad, gain_grad, gin_out, gout_out,
    win, wout, nf, ngp, ngt, cg, ab, aq, dg, px, rx1, rx2, po, ro1, ro2, acc, slope,
    pgi, pgo, gi1, gi2, go2, stat, tails, gains, wsem_in, wsem_out, osem, ssem, rsem,
):
    d, r, c = lax.axis_index("dp"), lax.axis_index("row"), lax.axis_index("col")
    zh, y = lax.div(d, 4), lax.rem(d, 4)
    zl, co = lax.div(r, 2), lax.rem(r, 2)
    cr, cl = lax.rem(c + 1, 4), lax.rem(c + 3, 4)
    yr, yl = lax.rem(y + 1, 4), lax.rem(y + 3, 4)
    cq, yq = lax.rem(c + 2, 4), lax.rem(y + 2, 4)
    XR, XL, XQ = (d, r, cr), (d, r, cl), (d, r, cq)
    YR, YL, YQ = (zh * 4 + yr, r, c), (zh * 4 + yl, r, c), (zh * 4 + yq, r, c)
    ZL, ZH = (d, (1 - zl) * 2 + co, c), ((1 - zh) * 4 + y, r, c)
    CO = (d, zl * 2 + 1 - co, c)
    YA = (zh * 4 + y + 1 - 2 * lax.rem(y, 2), r, c)
    YB = (zh * 4 + 3 - y, r, c)

    def slot(ref, i, first=0):
        return ref.at[pl.ds(first + 2 * (i % 2), 2), i // 2]

    count = [0]
    sends = []
    V = {"cot": {}}

    def rc(src, dst, dev):
        i = count[0]
        count[0] += 1
        cp = pltpu.make_async_remote_copy(
            src, dst, ssem.at[i], rsem.at[i], device_id=dev, device_id_type=MESH
        )
        cp.start()
        sends.append(cp)
        return cp

    def recv(*cps):
        for cp in cps:
            cp.wait_recv()

    def drain(cps):
        for cp in cps:
            cp.wait_send()
        gone = [id(cp) for cp in cps]
        sends[:] = [cp for cp in sends if id(cp) not in gone]

    def place(k):
        return 2 * lax.rem(k, 4) + lax.div(k, 4)

    def win_copy(j, k):
        return pltpu.make_async_copy(
            win_hbm.at[:, rows(k * 384 + j * 128, 128, 128)],
            win.at[j, :, rows(place(k) * 128, 128, 128)],
            wsem_in.at[j, k],
        )

    def wout_copy(j, k):
        return pltpu.make_async_copy(
            wout_hbm.at[rows(k * 384 + j * 128, 128, 128)],
            wout.at[j, rows(place(k) * 128, 128, 128)],
            wsem_out.at[j, k],
        )

    for j in range(NC):

        @pl.loop(0, 8)
        def _(k):
            wout_copy(j, k).start()
            win_copy(j, k).start()

    loaded = []

    def need(copy, key, j):
        if (key, j) not in loaded:
            loaded.append((key, j))

            @pl.loop(0, 8)
            def _(k):
                copy(j, k).wait()

    barrier = pltpu.get_barrier_semaphore()
    for dev in (XR, XL, XQ, YR, YL, YQ, ZL, ZH, CO):
        pl.semaphore_signal(barrier, inc=1, device_id=dev, device_id_type=MESH)

    cg[0, 0:2, 0] = cot[...].reshape(2, HALF, W)
    x = tok[...].astype(F32)
    lane = lax.broadcasted_iota(jnp.int32, (T, 128), 1)

    def two(a, b):
        return jnp.where(lane == 0, a, jnp.where(lane == 1, b, 0.0))

    stat[0] = two(jnp.sum(x, axis=1, keepdims=True), jnp.sum(x * x, axis=1, keepdims=True))
    pl.semaphore_wait(barrier, 9)

    def mean_inverse():
        mean = stat[4, :, 0:1] / MODEL_WIDTH
        return mean, lax.rsqrt(stat[4, :, 1:2] / MODEL_WIDTH - mean * mean + EPS)

    S = {}

    def spread(key, ref, first=0):
        own = slot(ref, 0, first)
        V[key] = {0: rc(own, slot(ref, 1, first), CO), 1: rc(own, slot(ref, 2, first), ZL)}

    def spread_on(key, ref, first=0):
        recv(V[key][1])
        V[key][2] = rc(slot(ref, 2, first), slot(ref, 3, first), CO)

    done = []

    def once(key, *cps):
        if key not in done:
            done.append(key)
            recv(*cps)

    def own_chip(key):
        once(key + "0", V[key][0])

    def whole(key):
        own_chip(key)
        once(key + "1", V[key][2])

    def cotc():
        V["cot"][0] = rc(slot(cg.at[0], 0), slot(cg.at[0], 1), CO)

    def cotz():
        V["cot"][1] = rc(slot(cg.at[0], 0), slot(cg.at[0], 2), ZL)

    S["cotc"], S["cotz"] = cotc, cotz
    S["cotf"] = lambda: spread_on("cot", cg.at[0])

    def to_column(key, ref):
        V[key] = [rc(ref.at[0], ref.at[1 + i], dev) for i, dev in enumerate((XR, XL, XQ))]

    def of_column(key, ref):
        recv(*V[key])
        ref[4] = (ref[0] + ref[3]) + (ref[1] + ref[2])

    def st1():
        to_column("sa", stat)

    def st3():
        of_column("sa", stat)
        mean, inverse = mean_inverse()
        normed = ((tok[...].astype(F32) - mean) * inverse * gain[...].reshape(1, W)).astype(BF16)
        nf[0:2, 0] = normed.reshape(2, HALF, W)
        spread("nor", nf)

    S["st1"], S["st3"] = st1, st3
    S["norf"] = lambda: spread_on("nor", nf)

    def norh():
        V["norh"] = rc(
            nf.at[0:2, 0, :, rows((1 - zh) * FG, FG, 128)], slot(ngp, 0), ZH
        )

    def nph():
        recv(V["norh"])
        spread("np", ngp)

    def ngt0():
        whole("nor")
        ngt[:, 0:G] = jnp.transpose(nf[:, :, :, rows(zh * FG, FG, 128)].reshape(G, FG))

    def ngt1():
        whole("np")
        ngt[:, G:] = jnp.transpose(ngp[...].reshape(G, FG))

    S["norh"], S["nph"] = norh, nph
    S["ngt0"], S["ngt1"] = ngt0, ngt1

    def round_y(key, half):
        own = cg.at[0, 0:2, half]
        V[key] = [rc(own, cg.at[3, 0:2, half], YR), rc(own, cg.at[1, 0:2, half], YL)]

    def round_y_on(key, half):
        recv(V[key][0])
        V[key].append(rc(cg.at[3, 0, half], cg.at[2, 0, half], YR))
        recv(V[key][1])
        V[key].append(rc(cg.at[1, 1, half], cg.at[2, 1, half], YL))

    def cyc():
        recv(*V["cya"][2:], *V["cyb"][2:])
        V["cyc"] = rc(cg.at[1:4, 0:2], cg.at[1:4, 2:4], CO)

    S["cya"] = lambda: round_y("cya", 0)
    S["cyaf"] = lambda: round_y_on("cya", 0)
    S["cyb"] = lambda: round_y("cyb", 1)
    S["cybf"] = lambda: round_y_on("cyb", 1)
    S["cyc"] = cyc
    S["npf"] = lambda: spread_on("np", ngp)

    def add(part, buf):
        part[...] = (part[...].astype(F32) + buf[...].astype(F32)).astype(BF16)

    CA, CB = pl.ds(0, H // 2), pl.ds(H // 2, H // 2)

    def product(kind, j, h):
        key = "cot" if kind == 0 else "nor"
        (need(wout_copy, "o", j) if kind == 0 else need(win_copy, "i", j))
        own_chip(key) if h == 0 else whole(key)
        if j >= 2 and h != 1:
            drain(V["x1", kind, j - 2] + V["x2", kind, j - 2])
        src = cg.at[0] if kind == 0 else nf
        part = px.at[kind, j % 2]

        @pl.loop(0, H // 256)
        def _(n):
            at = rows(n * 256, 256, 256)
            if h is None:
                left = src[...].reshape(G, W)
            else:
                left = src[:, h].reshape(G // 2, W)
            if kind == 0:
                out = lax.dot_general(left, wout[j, at], LAST, preferred_element_type=F32)
            else:
                out = jnp.dot(left, win[j, :, at], preferred_element_type=F32)
            if h is None:
                part[:, :, :, at] = out.astype(BF16).reshape(4, 2, HALF, 256)
            else:
                part[:, h, :, at] = out.astype(BF16).reshape(4, HALF, 256)

        buf = rx1.at[kind, j]
        if h is None:
            new = [rc(part.at[cq, 0], buf.at[0], XR), rc(part.at[cq, 1], buf.at[1], XL)]
        else:
            new = [
                rc(part.at[cq, h, :, CA], buf.at[h, :, CA], XR),
                rc(part.at[cq, h, :, CB], buf.at[h, :, CB], XL),
            ]
        V["x1", kind, j, h] = new
        V["x1", kind, j] = V.get(("x1", kind, j), []) + new

    def second(kind, j, h):
        one, other = V["x1", kind, j, h]
        part, buf, out = px.at[kind, j % 2], rx1.at[kind, j], rx2.at[kind, j]
        new = []
        if h is None:
            recv(one)
            add(part.at[cr, 0], buf.at[0])
            new.append(rc(part.at[cr], out.at[0], XR))
            recv(other)
            add(part.at[cl, 1], buf.at[1])
            new.append(rc(part.at[cl], out.at[1], XL))
        else:
            recv(one)
            add(part.at[cr, h, :, CA], buf.at[h, :, CA])
            new.append(rc(part.at[cr, h], out.at[0, h], XR))
            recv(other)
            add(part.at[cl, h, :, CB], buf.at[h, :, CB])
            new.append(rc(part.at[cl, h], out.at[1, h], XL))
        V["x2", kind, j, h] = new
        V["x2", kind, j] = V.get(("x2", kind, j), []) + new

    def total(kind, j, h, at):
        here = slice(None) if h is None else h
        return (
            px[kind, j % 2, c, here, :, at].astype(F32)
            + rx2[kind, j, 0, here, :, at].astype(F32)
            + rx2[kind, j, 1, here, :, at].astype(F32)
        ).reshape(T if h is None else HALF, 256)

    def arrived(kind, j, h):
        split = j in (SPLIT_DACT, SPLIT_PRE)[kind]
        for part in ((0, 1) if h is None else (h,)) if split else (None,):
            once(("x2", kind, j, part), *V["x2", kind, j, part])

    def own_rows(h):
        return rows(c * T, T) if h is None else rows(c * T + h * HALF, HALF)

    def activate(j, h):
        arrived(1, j, h)
        to = slice(0, T) if h is None else slice(h * HALF, (h + 1) * HALF)

        @pl.loop(0, H // 256)
        def _(n):
            at = rows(n * 256, 256, 256)
            pre = total(1, j, h, at)
            cdf = 0.5 * (1.0 + lax.erf(pre * 0.7071067811865476))
            dens = jnp.exp(-0.5 * pre * pre) * 0.3989422804014327
            ab[j, own_rows(h), at] = (pre * cdf).astype(BF16)
            slope[j % 2, to, at] = cdf + pre * dens

        both_ways(("a", j, h), ab.at[j], 0, h)

    def dgelu(j, h):
        arrived(0, j, h)
        to = slice(0, T) if h is None else slice(h * HALF, (h + 1) * HALF)

        @pl.loop(0, H // 256)
        def _(n):
            at = rows(n * 256, 256, 256)
            dg[j, own_rows(h), at] = (total(0, j, h, at) * slope[j % 2, to, at]).astype(BF16)

        both_ways(("d", j, h), dg.at[j], 0, h)

    def both_ways(key, ref, base, h=None):
        own = ref.at[rows(base + c * T, T) if h is None else rows(base + c * T + h * HALF, HALF)]
        V[key] = [rc(own, own, XR), rc(own, own, XL)]

    def forward(key, ref, base, h=None):
        one, other = V[key]
        once((key, 0), one)
        if h is None:
            a = ref.at[rows(base + cl * T, HALF)]
            b = ref.at[rows(base + cr * T + HALF, HALF)]
        else:
            a = ref.at[rows(base + cl * T + h * HALF, HALF), CA]
            b = ref.at[rows(base + cr * T + h * HALF, HALF), CB]
        V[key].append(rc(a, a, XR))
        once((key, 1), other)
        V[key].append(rc(b, b, XL))

    def ends(key):
        once((key, 2), V[key][2])
        once((key, 3), V[key][3])

    def halves(j):
        return ((0, "a"), (1, "b")) if j in SPLIT_ACT else ((None, ""),)

    def all_ends(kind, j):
        for h, _ in halves(j):
            ends((kind, j, h))

    def over_z(j, piece):
        return rc(dg.at[j, rows(piece * T, T)], dg.at[j, rows(G + piece * T, T)], ZH)

    def partner_steps(j, way):
        key = ("dp", j)

        def z_own():
            V["z", j] = over_z(j, c)

        S["zd%d" % j] = z_own

        def over_x():
            once(("z", j), V["z", j])
            both_ways(key, dg.at[j], G)

        def opposite():
            all_ends("d", j)
            V["zq", j] = over_z(j, cq)

        def neighbours():
            for h, _ in halves(j):
                for i in (0, 1):
                    once((("d", j, h), i), V["d", j, h][i])
            V["zn", j] = [over_z(j, cl), over_z(j, cr)]

        if way < 4:
            S["dp%d" % j] = over_x
        if way == 1:
            S["dpf%d" % j] = lambda: forward(key, dg.at[j], G)
        if way > 1:
            S["zdq%d" % j] = opposite
        if way == 4:
            S["zdn%d" % j] = neighbours

        def wait():
            if way == 1:
                ends(key)
            elif way == 2:
                recv(*V[key], V["zq", j])
            else:
                recv(V["z", j], *V["zn", j], V["zq", j])

        return wait

    ocps = []

    def out_copy(key, j, k):
        if key == "o":
            return pltpu.make_async_copy(
                pgo.at[j, 1], gout_out.at[0, pl.ds(j * 128, 128)], osem.at[0, j, 0]
            )
        return pltpu.make_async_copy(
            gi2.at[j, 0, :, pl.ds((2 * (k % 4) + k // 4) * 128, 128)],
            gin_out.at[0, :, pl.ds(k * 384 + j * 128, 128)],
            osem.at[1, j, k],
        )

    def grad_out_steps(j):
        def spread_act():
            all_ends("a", j)
            V["ya", j] = [
                rc(ab.at[j, :, rows(to * 256, 256, 256)], aq.at[j, i], dev)
                for to, i, dev in ((yr, 3, YR), (yl, 1, YL), (yq, 2, YQ))
            ]

        def block(z):
            at = rows(z * 128, 128, 128)
            return lax.dot_general(
                aq[j, :, :, at].reshape(4 * G, 128),
                cg[...].reshape(4 * G, W),
                FIRST,
                preferred_element_type=F32,
            ).astype(BF16)

        def compute():
            all_ends("a", j)
            aq[j, 0] = ab[j, :, rows(y * 256, 256, 256)]
            recv(*V["ya", j])
            once("cyc", V["cyc"])
            pgo[j, 0] = block(1 - zh)
            V["o", j] = rc(pgo.at[j, 0], go2.at[j], ZH)
            pgo[j, 1] = block(zh)

        def end():
            recv(V["o", j])
            add(pgo.at[j, 1], go2.at[j])
            cp = out_copy("o", j, 0)
            cp.start()
            ocps.append(cp)

        S["ya%d" % j], S["go%d" % j], S["geo%d" % j] = spread_act, compute, end

    def gradient_steps(key, j, wait, split):
        part, b1, b2, size = pgi.at[j % 2], gi1.at[j], gi2.at[j], FB
        pieces = (("a", 0), ("b", 1)) if split else (("", 0),)
        ps = size // len(pieces)
        h = ps // 2

        def block(b):
            at = rows(b * size, size)
            part[at] = jnp.dot(ngt[at], dg[j], preferred_element_type=F32).astype(BF16)

        def compute():
            all_ends("d", j)
            wait()
            if j >= 2:
                drain(V["y", key, j - 2])
            block(yq)
            V["y", key, j] = []
            for name, p in pieces:
                new = [
                    rc(part.at[rows(yq * size + p * ps, h)], b1.at[rows(2 * p * h, h)], YR),
                    rc(part.at[rows(yq * size + p * ps + h, h)], b1.at[rows(2 * p * h + h, h)], YL),
                ]
                V["y1", key, j, name] = new
                V["y", key, j] += new

            @pl.loop(1, 4)
            def _(i):
                block(lax.rem(yq + i, 4))

        S["g%s%d" % (key, j)] = compute

        def piece_steps(name, p):
            def on():
                one, other = V["y1", key, j, name]
                recv(one)
                add(part.at[rows(yr * size + p * ps, h)], b1.at[rows(2 * p * h, h)])
                new = [rc(part.at[rows(yr * size + p * ps, ps)], b2.at[0, rows(p * ps, ps)], YR)]
                recv(other)
                add(part.at[rows(yl * size + p * ps + h, h)], b1.at[rows(2 * p * h + h, h)])
                new.append(rc(part.at[rows(yl * size + p * ps, ps)], b2.at[1, rows(p * ps, ps)], YL))
                V["y2", key, j, name] = new
                V["y", key, j] += new

            def end():
                recv(*V["y2", key, j, name])
                at = rows(p * ps, ps)
                b2[0, at] = (
                    part[rows(y * size + p * ps, ps)].astype(F32)
                    + b2[0, at].astype(F32)
                    + b2[1, at].astype(F32)
                ).astype(BF16)
                V["left", key, j] = V.get(("left", key, j), len(pieces)) - 1
                if V["left", key, j] == 0:
                    for k in range(8):
                        cp = out_copy(key, j, k)
                        cp.start()
                        ocps.append(cp)

            S["gs%s%d%s" % (key, j, name)] = on
            S["ge%s%d%s" % (key, j, name)] = end

        for name, p in pieces:
            piece_steps(name, p)

    def chunk_steps(j):
        for kind, name, k, split in (
            (0, "dact", "d", j in SPLIT_DACT),
            (1, "pre", "p", j in SPLIT_PRE),
        ):
            for h, tail in ((0, "a"), (1, "b")) if split else ((None, ""),):
                S["%s%d%s" % (name, j, tail)] = lambda kind=kind, h=h: product(kind, j, h)
                S["rs%s%d%s" % (k, j, tail)] = lambda kind=kind, h=h: second(kind, j, h)
        for h, tail in halves(j):
            S["act%d%s" % (j, tail)] = lambda h=h: activate(j, h)
            S["dgr%d%s" % (j, tail)] = lambda h=h: dgelu(j, h)
            S["af%d%s" % (j, tail)] = lambda h=h: forward(("a", j, h), ab.at[j], 0, h)
            S["df%d%s" % (j, tail)] = lambda h=h: forward(("d", j, h), dg.at[j], 0, h)
        grad_out_steps(j)
        gradient_steps("i", j, partner_steps(j, DPRE_WAY[j]), j in SPLIT_IN)

    for j in range(NC):
        chunk_steps(j)

    def out():
        for j in range(NC):
            all_ends("a", j)

        @pl.loop(0, W // 256)
        def _(n):
            at = rows(n * 256, 256, 256)
            total = jnp.dot(ab[0], wout[0, :, at], preferred_element_type=F32)
            for j in range(1, NC):
                total += jnp.dot(ab[j], wout[j, :, at], preferred_element_type=F32)
            po[0, :, :, :, at] = total.astype(BF16).reshape(4, 2, HALF, 256)

        V["lo1"] = rc(po.at[0, 2:4], ro1.at[0], CO)

    def dna():
        for j in (0, 1):
            all_ends("d", j)

        @pl.loop(0, W // 256)
        def _(n):
            at = rows(n * 256, 256, 256)
            acc[:, at] = sum(
                lax.dot_general(dg[j, 0:G], win[j, at], LAST, preferred_element_type=F32)
                for j in (0, 1)
            )

    def dnb():
        all_ends("d", 2)

        @pl.loop(0, W // 256)
        def _(n):
            at = rows(n * 256, 256, 256)
            total = acc[:, at] + lax.dot_general(
                dg[2, 0:G], win[2, at], LAST, preferred_element_type=F32
            )
            po[1, :, :, :, at] = total.astype(BF16).reshape(4, 2, HALF, 256)

        V["dn1"] = rc(po.at[1, 2:4], ro1.at[1], CO)

    def row_second(q, key):
        recv(V[key])
        add(po.at[q, 0:2, 1], ro1.at[q, :, 1])
        return rc(po.at[q, 0:2, 1], ro2.at[q], ZL)

    def row_sum(q):
        return (
            po[q, 0:2, 0].astype(F32) + ro1[q, :, 0].astype(F32) + ro2[q].astype(F32)
        ).reshape(T, W)

    def lo2():
        V["lo2"] = row_second(0, "lo1")

    def dn2():
        V["dn2"] = row_second(1, "dn1")

    def lo3():
        recv(V["lo2"])
        layer_out[...] = (tok[...].astype(F32) + row_sum(0)).astype(BF16)

    def fin():
        recv(V["dn2"])
        mean, inverse = mean_inverse()
        dnorm = row_sum(1)
        xhat = (tok[...].astype(F32) - mean) * inverse
        gains[0] = jnp.sum((dnorm * xhat).reshape(T // 8, 8, W), axis=0)
        V["ga"] = rc(gains.at[0], gains.at[1], CO)
        dxhat = dnorm * gain[...].reshape(1, W)
        tails[0] = two(
            jnp.sum(dxhat, axis=1, keepdims=True), jnp.sum(dxhat * xhat, axis=1, keepdims=True)
        )
        to_column("ta", tails)

    def t3():
        of_column("ta", tails)
        mean, inverse = mean_inverse()
        first = tails[4, :, 0:1] / MODEL_WIDTH
        second = tails[4, :, 1:2] / MODEL_WIDTH
        xhat = (tok[...].astype(F32) - mean) * inverse
        token_grad[...] = (
            cot[...].astype(F32) + inverse * (row_sum(1) * gain[...].reshape(1, W) - first - xhat * second)
        ).astype(BF16)

    def gain_step(i, old, new, dev):
        def step():
            recv(V[old])
            gains[2 * i + 2] = gains[2 * i] + gains[2 * i + 1]
            V[new] = rc(gains.at[2 * i + 2], gains.at[2 * i + 3], dev)

        return step

    def gz():
        recv(V["ge"])
        gain_grad[...] = jnp.sum(gains[8] + gains[9], axis=0)

    S.update(out=out, dna=dna, dnb=dnb, lo2=lo2, dn2=dn2, lo3=lo3, fin=fin, t3=t3, gz=gz)
    S["gb"] = gain_step(0, "ga", "gb", ZL)
    S["gc"] = gain_step(1, "gb", "gc", ZH)
    S["gd"] = gain_step(2, "gc", "gd", YA)
    S["ge"] = gain_step(3, "gd", "ge", YB)

    assert sorted(S) == sorted(ORDER)
    for name in ORDER:
        S[name]()
    drain(list(sends))
    for cp in ocps:
        cp.wait()
    assert count[0] <= N_COPIES, count[0]


N_COPIES = 230


def copy_kernel(*refs):
    src, dst, via, (one, two) = refs[:5], refs[5:10], refs[10:15], refs[15:]
    first = [pltpu.make_async_copy(src[i], via[i], one.at[i]) for i in range(5)]
    then = [pltpu.make_async_copy(via[i], dst[i], two.at[i]) for i in range(5)]
    for cp in first:
        cp.start()
    for a, b in zip(first, then):
        a.wait()
        b.start()
    for cp in then:
        cp.wait()


def body(tokens, norm_scale_gain, in_weight, out_weight, cotangent):
    vm = pl.BlockSpec(memory_space=pltpu.VMEM)
    hbm = pl.BlockSpec(memory_space=pl.ANY)
    layer_out, token_grad, gain_grad, grad_in, grad_out = pl.pallas_call(
        kernel,
        out_shape=(
            jax.ShapeDtypeStruct((T, W), BF16),
            jax.ShapeDtypeStruct((T, W), BF16),
            jax.ShapeDtypeStruct((W,), F32),
            jax.ShapeDtypeStruct((1, FB, NC * H), BF16),
            jax.ShapeDtypeStruct((1, NC * 128, W), BF16),
        ),
        in_specs=[vm, vm, hbm, hbm, vm],
        out_specs=(vm, vm, vm, hbm, hbm),
        scratch_shapes=[
            pltpu.VMEM((NC, W, H), BF16),
            pltpu.VMEM((NC, H, W), BF16),
            pltpu.VMEM((4, 2, HALF, W), BF16),
            pltpu.VMEM((4, 2, HALF, FG), BF16),
            pltpu.VMEM((FG, 2 * G), BF16),
            pltpu.VMEM((4, 4, 2, HALF, W), BF16),
            pltpu.VMEM((NC, G, H), BF16),
            pltpu.VMEM((NC, 4, G, 256), BF16),
            pltpu.VMEM((NC, 2 * G, H), BF16),
            pltpu.VMEM((2, 2, 4, 2, HALF, H), BF16),
            pltpu.VMEM((2, NC, 2, HALF, H), BF16),
            pltpu.VMEM((2, NC, 2, 2, HALF, H), BF16),
            pltpu.VMEM((2, 4, 2, HALF, W), BF16),
            pltpu.VMEM((2, 2, 2, HALF, W), BF16),
            pltpu.VMEM((2, 2, HALF, W), BF16),
            pltpu.VMEM((G, W), F32),
            pltpu.VMEM((2, T, H), F32),
            pltpu.VMEM((2, FG, H), BF16),
            pltpu.VMEM((NC, 2, 128, W), BF16),
            pltpu.VMEM((NC, FB, H), BF16),
            pltpu.VMEM((NC, 2, FB, H), BF16),
            pltpu.VMEM((NC, 128, W), BF16),
            pltpu.VMEM((5, T, 128), F32),
            pltpu.VMEM((5, T, 128), F32),
            pltpu.VMEM((10, 8, W), F32),
            pltpu.SemaphoreType.DMA((NC, 8)),
            pltpu.SemaphoreType.DMA((NC, 8)),
            pltpu.SemaphoreType.DMA((2, NC, 8)),
            pltpu.SemaphoreType.DMA((N_COPIES,)),
            pltpu.SemaphoreType.DMA((N_COPIES,)),
        ],
        compiler_params=pltpu.CompilerParams(
            collective_id=0, has_side_effects=True, vmem_limit_bytes=63 * 2**20
        ),
        cost_estimate=pl.CostEstimate(
            flops=22 * 10**9, bytes_accessed=24 * 10**6, transcendentals=600000
        ),
        name="feed_forward",
    )(tokens, norm_scale_gain, in_weight, out_weight, cotangent)
    arrays = (layer_out, token_grad, gain_grad, grad_in, grad_out)
    return pl.pallas_call(
        copy_kernel,
        out_shape=tuple(jax.ShapeDtypeStruct(a.shape, a.dtype) for a in arrays),
        in_specs=[hbm] * 5,
        out_specs=(hbm,) * 5,
        scratch_shapes=[pltpu.VMEM(a.shape, a.dtype) for a in arrays]
        + [pltpu.SemaphoreType.DMA((5,)), pltpu.SemaphoreType.DMA((5,))],
        name="results",
    )(*arrays)


def solution(mesh):
    in_specs = (
        P(("dp", "row"), "col"),
        P("col"),
        P("col", "row"),
        P("row", "col"),
        P(("dp", "row"), "col"),
    )
    out_specs = (
        P(("dp", "row"), "col"),
        P(("dp", "row"), "col"),
        P("col"),
        P("dp", "col", "row"),
        P("dp", "row", "col"),
    )
    return jax.shard_map(body, mesh=mesh, in_specs=in_specs, out_specs=out_specs, check_vma=False)
```

```python
import jax
import jax.numpy as jnp
from jax import lax
from jax.experimental import pallas as pl
from jax.experimental.pallas import tpu as pltpu
from jax.sharding import PartitionSpec as P

MODEL_WIDTH = 6144
EPS = 1e-06
MESH = pl.DeviceIdType.MESH
F32 = jnp.float32
BF16 = jnp.bfloat16

T = 96
G = 384
W = 1536
H = 1024
NC = 3
HALF = T // 2
FB = 192
FG = 4 * FB
LAST = (((1,), (1,)), ((), ()))
FIRST = (((0,), (0,)), ((), ()))

DPRE_WAY = (4, 4, 2)
SPLIT_DACT = (0, 1)
SPLIT_PRE = (0,)
SPLIT_IN = (2,)
SPLIT_ACT = (0,)

ORDER = (
    "cotc", "cotz", "st1", "cya", "dact0a", "dact1a", "st3", "rsd0a", "pre0a", "cotf", "rsd1a",
    "dact0b", "rsp0a", "dact1b", "norh", "cyaf", "cyb", "norf", "rsd0b", "pre0b", "act0a", "rsp0b",
    "af0a", "nph", "dgr0a", "act0b", "dgr0b", "zd0", "cybf", "pre1", "af0b", "zdn0", "npf", "df0b",
    "df0a", "cyc", "rsp1", "rsd1b", "ya0", "ngt0", "zdq0", "pre2", "ngt1", "act1", "dgr1", "zd1",
    "dact2", "go0", "af1", "gi0", "zdn1", "df1", "rsp2", "ya1", "zdq1", "rsd2", "dna", "gsi0",
    "act2", "dgr2", "zd2", "go1", "gi1", "af2", "df2", "dp2", "ya2", "zdq2", "dnb", "dn2", "gei0",
    "gsi1", "gi2", "go2", "out", "fin", "gsi2a", "gb", "lo2", "gsi2b", "t3", "gei1", "geo0",
    "gei2a", "gc", "geo1", "gei2b", "geo2", "gz", "lo3",
)


def rows(start, size, unit=16):
    return pl.ds(pl.multiple_of(start, unit), size)


def kernel(
    tok, gain, win_hbm, wout_hbm, cot,
    layer_out, token_grad, gain_grad, gin_out, gout_out,
    win, wout, nf, ngp, ngt, cg, ab, aq, dg, px, rx1, rx2, po, ro1, ro2, acc, slope,
    pgi, pgo, gi1, gi2, go2, stat, tails, sums, gains, result, wsem_in, wsem_out, osem, rsem_out, ssem, rsem,
):
    d, r, c = lax.axis_index("dp"), lax.axis_index("row"), lax.axis_index("col")
    zh, y = lax.div(d, 4), lax.rem(d, 4)
    zl, co = lax.div(r, 2), lax.rem(r, 2)
    cr, cl = lax.rem(c + 1, 4), lax.rem(c + 3, 4)
    yr, yl = lax.rem(y + 1, 4), lax.rem(y + 3, 4)
    cq, yq = lax.rem(c + 2, 4), lax.rem(y + 2, 4)
    XR, XL, XQ = (d, r, cr), (d, r, cl), (d, r, cq)
    YR, YL, YQ = (zh * 4 + yr, r, c), (zh * 4 + yl, r, c), (zh * 4 + yq, r, c)
    ZL, ZH = (d, (1 - zl) * 2 + co, c), ((1 - zh) * 4 + y, r, c)
    CO, ZLO = (d, zl * 2 + 1 - co, c), (d, (1 - zl) * 2 + 1 - co, c)

    def slot(ref, i, first=0):
        return ref.at[pl.ds(first + 2 * (i % 2), 2), i // 2]

    count = [0]
    sends = []
    V = {"cot": {}}

    def rc(src, dst, dev):
        i = count[0]
        count[0] += 1
        cp = pltpu.make_async_remote_copy(
            src, dst, ssem.at[i], rsem.at[i], device_id=dev, device_id_type=MESH
        )
        cp.start()
        sends.append(cp)
        return cp

    def recv(*cps):
        for cp in cps:
            cp.wait_recv()

    def drain(cps):
        gone = [id(cp) for cp in cps]
        for cp in sends:
            if id(cp) in gone:
                cp.wait_send()
        sends[:] = [cp for cp in sends if id(cp) not in gone]

    barrier = pltpu.get_barrier_semaphore()
    for dev in (XR, XL, XQ, YR, YL, YQ, ZL, ZLO, ZH, CO):
        pl.semaphore_signal(barrier, inc=1, device_id=dev, device_id_type=MESH)

    def place(k):
        return 2 * lax.rem(k, 4) + lax.div(k, 4)

    def win_copy(j, k):
        return pltpu.make_async_copy(
            win_hbm.at[:, rows(k * 384 + j * 128, 128, 128)],
            win.at[j, :, rows(place(k) * 128, 128, 128)],
            wsem_in.at[j, k],
        )

    def wout_copy(j, k):
        return pltpu.make_async_copy(
            wout_hbm.at[rows(k * 384 + j * 128, 128, 128)],
            wout.at[j, rows(place(k) * 128, 128, 128)],
            wsem_out.at[j, k],
        )

    def load(j):
        @pl.loop(0, 8)
        def _(k):
            wout_copy(j, k).start()
            win_copy(j, k).start()

    loaded = []

    def need(copy, key, j):
        if (key, j) not in loaded:
            loaded.append((key, j))

            @pl.loop(0, 8)
            def _(k):
                copy(j, k).wait()

    cg[0, 0:2, 0] = cot[...].reshape(2, HALF, W)
    load(0)
    x = tok[...].astype(F32)
    lane = lax.broadcasted_iota(jnp.int32, (T, 128), 1)

    def two_rows(a, b):
        both = jnp.where(lane == 0, a, jnp.where(lane == 1, b, 0.0))
        both = jnp.concatenate([both, jnp.zeros((128 - T, 128), F32)], axis=0)
        return jnp.transpose(both)[0:8]

    def two_columns(both):
        both = jnp.concatenate([both, jnp.zeros((120, 128), F32)], axis=0)
        return jnp.transpose(both)[0:T]

    stat[0] = two_rows(jnp.sum(x, axis=1, keepdims=True), jnp.sum(x * x, axis=1, keepdims=True))
    pl.semaphore_wait(barrier, 10)

    def mean_inverse():
        mean = sums[0, :, 0:1] / MODEL_WIDTH
        return mean, lax.rsqrt(sums[0, :, 1:2] / MODEL_WIDTH - mean * mean + EPS)

    S = {}

    def spread(key, ref, first=0):
        own = slot(ref, 0, first)
        V[key] = {0: rc(own, slot(ref, 1, first), CO), 1: rc(own, slot(ref, 2, first), ZL)}

    def spread_on(key, ref, first=0):
        recv(V[key][1])
        V[key][2] = rc(slot(ref, 2, first), slot(ref, 3, first), CO)

    done = []

    def once(key, *cps):
        if key not in done:
            done.append(key)
            recv(*cps)

    def own_chip(key):
        once(key + "0", V[key][0])

    def whole(key):
        own_chip(key)
        once(key + "1", V[key][2])

    def cotc():
        V["cot"][0] = rc(slot(cg.at[0], 0), slot(cg.at[0], 1), CO)

    def cotz():
        V["cot"][1] = rc(slot(cg.at[0], 0), slot(cg.at[0], 2), ZL)

    S["cotc"], S["cotz"] = cotc, cotz
    S["cotf"] = lambda: spread_on("cot", cg.at[0])

    def to_column(key, ref):
        V[key] = [rc(ref.at[0], ref.at[1 + i], dev) for i, dev in enumerate((XR, XL, XQ))]

    def of_column(key, ref, i):
        recv(*V[key])
        sums[i] = two_columns((ref[0] + ref[3]) + (ref[1] + ref[2]))

    def st1():
        to_column("sa", stat)
        for j in range(1, NC):
            load(j)

    def st3():
        of_column("sa", stat, 0)
        mean, inverse = mean_inverse()
        normed = ((tok[...].astype(F32) - mean) * inverse * gain[...].reshape(1, W)).astype(BF16)
        nf[0:2, 0] = normed.reshape(2, HALF, W)
        spread("nor", nf)

    S["st1"], S["st3"] = st1, st3
    S["norf"] = lambda: spread_on("nor", nf)

    def norh():
        V["norh"] = rc(
            nf.at[0:2, 0, :, rows((1 - zh) * FG, FG, 128)], slot(ngp, 0), ZH
        )

    def nph():
        recv(V["norh"])
        spread("np", ngp)

    def ngt0():
        whole("nor")
        ngt[:, 0:G] = jnp.transpose(nf[:, :, :, rows(zh * FG, FG, 128)].reshape(G, FG))

    def ngt1():
        whole("np")
        ngt[:, G:] = jnp.transpose(ngp[...].reshape(G, FG))

    S["norh"], S["nph"] = norh, nph
    S["ngt0"], S["ngt1"] = ngt0, ngt1

    def round_y(key, half):
        own = cg.at[0, 0:2, half]
        V[key] = [rc(own, cg.at[3, 0:2, half], YR), rc(own, cg.at[1, 0:2, half], YL)]

    def round_y_on(key, half):
        recv(V[key][0])
        V[key].append(rc(cg.at[3, 0, half], cg.at[2, 0, half], YR))
        recv(V[key][1])
        V[key].append(rc(cg.at[1, 1, half], cg.at[2, 1, half], YL))

    def cyc():
        recv(*V["cya"][2:], *V["cyb"][2:])
        V["cyc"] = rc(cg.at[1:4, 0:2], cg.at[1:4, 2:4], CO)

    S["cya"] = lambda: round_y("cya", 0)
    S["cyaf"] = lambda: round_y_on("cya", 0)
    S["cyb"] = lambda: round_y("cyb", 1)
    S["cybf"] = lambda: round_y_on("cyb", 1)
    S["cyc"] = cyc
    S["npf"] = lambda: spread_on("np", ngp)

    def add(part, buf):
        part[...] = (part[...].astype(F32) + buf[...].astype(F32)).astype(BF16)

    CA, CB = pl.ds(0, H // 2), pl.ds(H // 2, H // 2)

    def product(kind, j, h):
        key = "cot" if kind == 0 else "nor"
        (need(wout_copy, "o", j) if kind == 0 else need(win_copy, "i", j))
        own_chip(key) if h == 0 else whole(key)
        if j >= 2 and h != 1:
            drain(V["x1", kind, j - 2] + V["x2", kind, j - 2])
        src = cg.at[0] if kind == 0 else nf
        part = px.at[kind, j % 2]

        @pl.loop(0, H // 256)
        def _(n):
            at = rows(n * 256, 256, 256)
            if h is None:
                left = src[...].reshape(G, W)
            else:
                left = src[:, h].reshape(G // 2, W)
            if kind == 0:
                out = lax.dot_general(left, wout[j, at], LAST, preferred_element_type=F32)
            else:
                out = jnp.dot(left, win[j, :, at], preferred_element_type=F32)
            if h is None:
                part[:, :, :, at] = out.astype(BF16).reshape(4, 2, HALF, 256)
            else:
                part[:, h, :, at] = out.astype(BF16).reshape(4, HALF, 256)

        buf = rx1.at[kind, j]
        if h is None:
            new = [rc(part.at[cq, 0], buf.at[0], XR), rc(part.at[cq, 1], buf.at[1], XL)]
        else:
            new = [
                rc(part.at[cq, h, :, CA], buf.at[h, :, CA], XR),
                rc(part.at[cq, h, :, CB], buf.at[h, :, CB], XL),
            ]
        V["x1", kind, j, h] = new
        V["x1", kind, j] = V.get(("x1", kind, j), []) + new

    def second(kind, j, h):
        one, other = V["x1", kind, j, h]
        part, buf, out = px.at[kind, j % 2], rx1.at[kind, j], rx2.at[kind, j]
        new = []
        if h is None:
            recv(one)
            add(part.at[cr, 0], buf.at[0])
            new.append(rc(part.at[cr], out.at[0], XR))
            recv(other)
            add(part.at[cl, 1], buf.at[1])
            new.append(rc(part.at[cl], out.at[1], XL))
        else:
            recv(one)
            add(part.at[cr, h, :, CA], buf.at[h, :, CA])
            new.append(rc(part.at[cr, h], out.at[0, h], XR))
            recv(other)
            add(part.at[cl, h, :, CB], buf.at[h, :, CB])
            new.append(rc(part.at[cl, h], out.at[1, h], XL))
        V["x2", kind, j, h] = new
        V["x2", kind, j] = V.get(("x2", kind, j), []) + new

    def total(kind, j, h, at):
        here = slice(None) if h is None else h
        return (
            px[kind, j % 2, c, here, :, at].astype(F32)
            + rx2[kind, j, 0, here, :, at].astype(F32)
            + rx2[kind, j, 1, here, :, at].astype(F32)
        ).reshape(T if h is None else HALF, 256)

    def arrived(kind, j, h):
        split = j in (SPLIT_DACT, SPLIT_PRE)[kind]
        for part in ((0, 1) if h is None else (h,)) if split else (None,):
            once(("x2", kind, j, part), *V["x2", kind, j, part])

    def own_rows(h):
        return rows(c * T, T) if h is None else rows(c * T + h * HALF, HALF)

    def activate(j, h):
        arrived(1, j, h)
        to = slice(0, T) if h is None else slice(h * HALF, (h + 1) * HALF)

        @pl.loop(0, H // 256)
        def _(n):
            at = rows(n * 256, 256, 256)
            pre = total(1, j, h, at)
            cdf = 0.5 * (1.0 + lax.erf(pre * 0.7071067811865476))
            dens = jnp.exp(-0.5 * pre * pre) * 0.3989422804014327
            ab[j, own_rows(h), at] = (pre * cdf).astype(BF16)
            slope[j % 2, to, at] = cdf + pre * dens

        both_ways(("a", j, h), ab.at[j], 0, h)

    def dgelu(j, h):
        arrived(0, j, h)
        to = slice(0, T) if h is None else slice(h * HALF, (h + 1) * HALF)

        @pl.loop(0, H // 256)
        def _(n):
            at = rows(n * 256, 256, 256)
            dg[j, own_rows(h), at] = (total(0, j, h, at) * slope[j % 2, to, at]).astype(BF16)

        both_ways(("d", j, h), dg.at[j], 0, h)

    def both_ways(key, ref, base, h=None):
        own = ref.at[rows(base + c * T, T) if h is None else rows(base + c * T + h * HALF, HALF)]
        V[key] = [rc(own, own, XR), rc(own, own, XL)]

    def forward(key, ref, base, h=None):
        one, other = V[key]
        once((key, 0), one)
        if h is None:
            a = ref.at[rows(base + cl * T, HALF)]
            b = ref.at[rows(base + cr * T + HALF, HALF)]
        else:
            a = ref.at[rows(base + cl * T + h * HALF, HALF), CA]
            b = ref.at[rows(base + cr * T + h * HALF, HALF), CB]
        V[key].append(rc(a, a, XR))
        once((key, 1), other)
        V[key].append(rc(b, b, XL))

    def ends(key):
        once((key, 2), V[key][2])
        once((key, 3), V[key][3])

    def halves(j):
        return ((0, "a"), (1, "b")) if j in SPLIT_ACT else ((None, ""),)

    def all_ends(kind, j):
        for h, _ in halves(j):
            ends((kind, j, h))

    def over_z(j, piece):
        return rc(dg.at[j, rows(piece * T, T)], dg.at[j, rows(G + piece * T, T)], ZH)

    def partner_steps(j, way):
        key = ("dp", j)

        def z_own():
            V["z", j] = over_z(j, c)

        S["zd%d" % j] = z_own

        def over_x():
            once(("z", j), V["z", j])
            both_ways(key, dg.at[j], G)

        def opposite():
            all_ends("d", j)
            V["zq", j] = over_z(j, cq)

        def neighbours():
            for h, _ in halves(j):
                for i in (0, 1):
                    once((("d", j, h), i), V["d", j, h][i])
            V["zn", j] = [over_z(j, cl), over_z(j, cr)]

        if way < 4:
            S["dp%d" % j] = over_x
        if way == 1:
            S["dpf%d" % j] = lambda: forward(key, dg.at[j], G)
        if way > 1:
            S["zdq%d" % j] = opposite
        if way == 4:
            S["zdn%d" % j] = neighbours

        def wait():
            if way == 1:
                ends(key)
            elif way == 2:
                recv(*V[key], V["zq", j])
            else:
                recv(V["z", j], *V["zn", j], V["zq", j])

        return wait

    ocps = []

    def out_copy(key, j, k):
        if key == "o":
            return pltpu.make_async_copy(
                pgo.at[j, 1], gout_out.at[0, pl.ds(j * 128, 128)], osem.at[0, j, 0]
            )
        return pltpu.make_async_copy(
            gi2.at[j, 0, :, pl.ds((2 * (k % 4) + k // 4) * 128, 128)],
            gin_out.at[0, :, pl.ds(k * 384 + j * 128, 128)],
            osem.at[1, j, k],
        )

    def grad_out_steps(j):
        def spread_act():
            all_ends("a", j)
            V["ya", j] = [
                rc(ab.at[j, :, rows(to * 256, 256, 256)], aq.at[j, i], dev)
                for to, i, dev in ((yr, 3, YR), (yl, 1, YL), (yq, 2, YQ))
            ]

        def block(z):
            at = rows(z * 128, 128, 128)
            return lax.dot_general(
                aq[j, :, :, at].reshape(4 * G, 128),
                cg[...].reshape(4 * G, W),
                FIRST,
                preferred_element_type=F32,
            ).astype(BF16)

        def compute():
            all_ends("a", j)
            aq[j, 0] = ab[j, :, rows(y * 256, 256, 256)]
            recv(*V["ya", j])
            once("cyc", V["cyc"])
            pgo[j, 0] = block(1 - zh)
            V["o", j] = rc(pgo.at[j, 0], go2.at[j], ZH)
            pgo[j, 1] = block(zh)

        def end():
            recv(V["o", j])
            add(pgo.at[j, 1], go2.at[j])
            cp = out_copy("o", j, 0)
            cp.start()
            ocps.append(cp)

        S["ya%d" % j], S["go%d" % j], S["geo%d" % j] = spread_act, compute, end

    def gradient_steps(key, j, wait, split):
        part, b1, b2, size = pgi.at[j % 2], gi1.at[j], gi2.at[j], FB
        pieces = (("a", 0), ("b", 1)) if split else (("", 0),)
        ps = size // len(pieces)
        h = ps // 2

        def block(b):
            at = rows(b * size, size)
            part[at] = jnp.dot(ngt[at], dg[j], preferred_element_type=F32).astype(BF16)

        def compute():
            all_ends("d", j)
            wait()
            if j >= 2:
                drain(V["y", key, j - 2])
            block(yq)
            V["y", key, j] = []
            for name, p in pieces:
                new = [
                    rc(part.at[rows(yq * size + p * ps, h)], b1.at[rows(2 * p * h, h)], YR),
                    rc(part.at[rows(yq * size + p * ps + h, h)], b1.at[rows(2 * p * h + h, h)], YL),
                ]
                V["y1", key, j, name] = new
                V["y", key, j] += new

            @pl.loop(1, 4)
            def _(i):
                block(lax.rem(yq + i, 4))

        S["g%s%d" % (key, j)] = compute

        def piece_steps(name, p):
            def on():
                one, other = V["y1", key, j, name]
                recv(one)
                add(part.at[rows(yr * size + p * ps, h)], b1.at[rows(2 * p * h, h)])
                new = [rc(part.at[rows(yr * size + p * ps, ps)], b2.at[0, rows(p * ps, ps)], YR)]
                recv(other)
                add(part.at[rows(yl * size + p * ps + h, h)], b1.at[rows(2 * p * h + h, h)])
                new.append(rc(part.at[rows(yl * size + p * ps, ps)], b2.at[1, rows(p * ps, ps)], YL))
                V["y2", key, j, name] = new
                V["y", key, j] += new

            def end():
                recv(*V["y2", key, j, name])
                at = rows(p * ps, ps)
                b2[0, at] = (
                    part[rows(y * size + p * ps, ps)].astype(F32)
                    + b2[0, at].astype(F32)
                    + b2[1, at].astype(F32)
                ).astype(BF16)
                V["left", key, j] = V.get(("left", key, j), len(pieces)) - 1
                if V["left", key, j] == 0:
                    for k in range(8):
                        cp = out_copy(key, j, k)
                        cp.start()
                        ocps.append(cp)

            S["gs%s%d%s" % (key, j, name)] = on
            S["ge%s%d%s" % (key, j, name)] = end

        for name, p in pieces:
            piece_steps(name, p)

    def chunk_steps(j):
        for kind, name, k, split in (
            (0, "dact", "d", j in SPLIT_DACT),
            (1, "pre", "p", j in SPLIT_PRE),
        ):
            for h, tail in ((0, "a"), (1, "b")) if split else ((None, ""),):
                S["%s%d%s" % (name, j, tail)] = lambda kind=kind, h=h: product(kind, j, h)
                S["rs%s%d%s" % (k, j, tail)] = lambda kind=kind, h=h: second(kind, j, h)
        for h, tail in halves(j):
            S["act%d%s" % (j, tail)] = lambda h=h: activate(j, h)
            S["dgr%d%s" % (j, tail)] = lambda h=h: dgelu(j, h)
            S["af%d%s" % (j, tail)] = lambda h=h: forward(("a", j, h), ab.at[j], 0, h)
            S["df%d%s" % (j, tail)] = lambda h=h: forward(("d", j, h), dg.at[j], 0, h)
        grad_out_steps(j)
        gradient_steps("i", j, partner_steps(j, DPRE_WAY[j]), j in SPLIT_IN)

    for j in range(NC):
        chunk_steps(j)

    def out():
        for j in range(NC):
            all_ends("a", j)

        @pl.loop(0, W // 256)
        def _(n):
            at = rows(n * 256, 256, 256)
            total = jnp.dot(ab[0], wout[0, :, at], preferred_element_type=F32)
            for j in range(1, NC):
                total += jnp.dot(ab[j], wout[j, :, at], preferred_element_type=F32)
            po[0, :, :, :, at] = total.astype(BF16).reshape(4, 2, HALF, 256)

        V["lo1"] = rc(po.at[0, 2:4], ro1.at[0], CO)

    def dna():
        for j in (0, 1):
            all_ends("d", j)

        @pl.loop(0, W // 256)
        def _(n):
            at = rows(n * 256, 256, 256)
            acc[:, at] = sum(
                lax.dot_general(dg[j, 0:G], win[j, at], LAST, preferred_element_type=F32)
                for j in (0, 1)
            )

    def dnb():
        all_ends("d", 2)

        @pl.loop(0, W // 256)
        def _(n):
            at = rows(n * 256, 256, 256)
            total = acc[:, at] + lax.dot_general(
                dg[2, 0:G], win[2, at], LAST, preferred_element_type=F32
            )
            po[1, :, :, :, at] = total.astype(BF16).reshape(4, 2, HALF, 256)

        V["dn1"] = rc(po.at[1, 2:4], ro1.at[1], CO)

    def row_second(q, key):
        recv(V[key])
        add(po.at[q, 0:2, 1], ro1.at[q, :, 1])
        return rc(po.at[q, 0:2, 1], ro2.at[q], ZL)

    def row_sum(q):
        return (
            po[q, 0:2, 0].astype(F32) + ro1[q, :, 0].astype(F32) + ro2[q].astype(F32)
        ).reshape(T, W)

    def lo2():
        V["lo2"] = row_second(0, "lo1")

    def dn2():
        V["dn2"] = row_second(1, "dn1")

    def leave(i, out):
        cp = pltpu.make_async_copy(result.at[i], out, rsem_out.at[i])
        cp.start()
        ocps.append(cp)

    def lo3():
        recv(V["lo2"])
        result[0] = (tok[...].astype(F32) + row_sum(0)).astype(BF16)
        leave(0, layer_out)

    def fin():
        recv(V["dn2"])
        mean, inverse = mean_inverse()
        dnorm = row_sum(1)
        xhat = (tok[...].astype(F32) - mean) * inverse
        gains[r] = jnp.sum(dnorm * xhat, axis=0, keepdims=True)
        V["ga"] = [rc(gains.at[r], gains.at[r], dev) for dev in (CO, ZL, ZLO)]
        dxhat = dnorm * gain[...].reshape(1, W)
        tails[0] = two_rows(
            jnp.sum(dxhat, axis=1, keepdims=True), jnp.sum(dxhat * xhat, axis=1, keepdims=True)
        )
        to_column("ta", tails)

    def t3():
        of_column("ta", tails, 1)
        mean, inverse = mean_inverse()
        first = sums[1, :, 0:1] / MODEL_WIDTH
        second = sums[1, :, 1:2] / MODEL_WIDTH
        xhat = (tok[...].astype(F32) - mean) * inverse
        result[1] = (
            cot[...].astype(F32) + inverse * (row_sum(1) * gain[...].reshape(1, W) - first - xhat * second)
        ).astype(BF16)
        leave(1, token_grad)

    def gb():
        recv(*V["ga"])
        gains[4 + zh] = (gains[0] + gains[1]) + (gains[2] + gains[3])
        V["gb"] = rc(gains.at[4 + zh], gains.at[4 + zh], ZH)

    def gc():
        recv(V["gb"])
        gains[6 + y] = gains[4] + gains[5]
        V["gc"] = [rc(gains.at[6 + y], gains.at[6 + y], dev) for dev in (YR, YL, YQ)]

    def gz():
        recv(*V["gc"])
        gain_grad[...] = jnp.sum((gains[6] + gains[7]) + (gains[8] + gains[9]), axis=0)

    S.update(out=out, dna=dna, dnb=dnb, lo2=lo2, dn2=dn2, lo3=lo3, fin=fin, t3=t3, gz=gz)
    S["gb"], S["gc"] = gb, gc

    assert sorted(S) == sorted(ORDER)
    for i, name in enumerate(ORDER):
        if i >= len(ORDER) - 12:
            drain(sends[:-16])
        S[name]()
    drain(list(sends))
    for cp in ocps:
        cp.wait()
    assert count[0] <= N_COPIES, count[0]


N_COPIES = 230


def copy_kernel(*refs):
    src, dst, via, (one, two) = refs[:5], refs[5:10], refs[10:15], refs[15:]
    first = [pltpu.make_async_copy(src[i], via[i], one.at[i]) for i in range(5)]
    then = [pltpu.make_async_copy(via[i], dst[i], two.at[i]) for i in range(5)]
    for cp in first:
        cp.start()
    for a, b in zip(first, then):
        a.wait()
        b.start()
    for cp in then:
        cp.wait()


def body(tokens, norm_scale_gain, in_weight, out_weight, cotangent):
    vm = pl.BlockSpec(memory_space=pltpu.VMEM)
    hbm = pl.BlockSpec(memory_space=pl.ANY)
    layer_out, token_grad, gain_grad, grad_in, grad_out = pl.pallas_call(
        kernel,
        out_shape=(
            jax.ShapeDtypeStruct((T, W), BF16),
            jax.ShapeDtypeStruct((T, W), BF16),
            jax.ShapeDtypeStruct((W,), F32),
            jax.ShapeDtypeStruct((1, FB, NC * H), BF16),
            jax.ShapeDtypeStruct((1, NC * 128, W), BF16),
        ),
        in_specs=[vm, vm, hbm, hbm, vm],
        out_specs=(hbm, hbm, vm, hbm, hbm),
        scratch_shapes=[
            pltpu.VMEM((NC, W, H), BF16),
            pltpu.VMEM((NC, H, W), BF16),
            pltpu.VMEM((4, 2, HALF, W), BF16),
            pltpu.VMEM((4, 2, HALF, FG), BF16),
            pltpu.VMEM((FG, 2 * G), BF16),
            pltpu.VMEM((4, 4, 2, HALF, W), BF16),
            pltpu.VMEM((NC, G, H), BF16),
            pltpu.VMEM((NC, 4, G, 256), BF16),
            pltpu.VMEM((NC, 2 * G, H), BF16),
            pltpu.VMEM((2, 2, 4, 2, HALF, H), BF16),
            pltpu.VMEM((2, NC, 2, HALF, H), BF16),
            pltpu.VMEM((2, NC, 2, 2, HALF, H), BF16),
            pltpu.VMEM((2, 4, 2, HALF, W), BF16),
            pltpu.VMEM((2, 2, 2, HALF, W), BF16),
            pltpu.VMEM((2, 2, HALF, W), BF16),
            pltpu.VMEM((G, W), F32),
            pltpu.VMEM((2, T, H), F32),
            pltpu.VMEM((2, FG, H), BF16),
            pltpu.VMEM((NC, 2, 128, W), BF16),
            pltpu.VMEM((NC, FB, H), BF16),
            pltpu.VMEM((NC, 2, FB, H), BF16),
            pltpu.VMEM((NC, 128, W), BF16),
            pltpu.VMEM((4, 8, 128), F32),
            pltpu.VMEM((4, 8, 128), F32),
            pltpu.VMEM((2, T, 128), F32),
            pltpu.VMEM((10, 1, W), F32),
            pltpu.VMEM((2, T, W), BF16),
            pltpu.SemaphoreType.DMA((NC, 8)),
            pltpu.SemaphoreType.DMA((NC, 8)),
            pltpu.SemaphoreType.DMA((2, NC, 8)),
            pltpu.SemaphoreType.DMA((2,)),
            pltpu.SemaphoreType.DMA((N_COPIES,)),
            pltpu.SemaphoreType.DMA((N_COPIES,)),
        ],
        compiler_params=pltpu.CompilerParams(
            collective_id=0, has_side_effects=True, vmem_limit_bytes=63 * 2**20
        ),
        cost_estimate=pl.CostEstimate(
            flops=22 * 10**9, bytes_accessed=24 * 10**6, transcendentals=600000
        ),
        name="feed_forward",
    )(tokens, norm_scale_gain, in_weight, out_weight, cotangent)
    arrays = (layer_out, token_grad, gain_grad, grad_in, grad_out)
    return pl.pallas_call(
        copy_kernel,
        out_shape=tuple(jax.ShapeDtypeStruct(a.shape, a.dtype) for a in arrays),
        in_specs=[hbm] * 5,
        out_specs=(hbm,) * 5,
        scratch_shapes=[pltpu.VMEM(a.shape, a.dtype) for a in arrays]
        + [pltpu.SemaphoreType.DMA((5,)), pltpu.SemaphoreType.DMA((5,))],
        name="results",
    )(*arrays)


def solution(mesh):
    in_specs = (
        P(("dp", "row"), "col"),
        P("col"),
        P("col", "row"),
        P("row", "col"),
        P(("dp", "row"), "col"),
    )
    out_specs = (
        P(("dp", "row"), "col"),
        P(("dp", "row"), "col"),
        P("col"),
        P("dp", "col", "row"),
        P("dp", "row", "col"),
    )
    return jax.shard_map(body, mesh=mesh, in_specs=in_specs, out_specs=out_specs, check_vma=False)
```

```python
import jax
import jax.numpy as jnp
from jax import lax
from jax.experimental import pallas as pl
from jax.experimental.pallas import tpu as pltpu
from jax.sharding import PartitionSpec as P

MODEL_WIDTH = 6144
EPS = 1e-06
MESH = pl.DeviceIdType.MESH
F32 = jnp.float32
BF16 = jnp.bfloat16

T = 96
G = 384
W = 1536
H = 1024
NC = 3
HALF = T // 2
FB = 192
FG = 4 * FB
LAST = (((1,), (1,)), ((), ()))
FIRST = (((0,), (0,)), ((), ()))

DPRE_WAY = (4, 4, 2)
SPLIT_DACT = (0, 1)
SPLIT_PRE = (0,)
SPLIT_IN = (2,)
SPLIT_ACT = (0,)

ORDER = (
    "cotc", "cotz", "st1", "dact0a", "dact1a", "st3", "rsd0a", "norh", "cya", "pre0a", "cotf",
    "rsd1a", "dact0b", "cyb", "dact1b", "rsp0a", "norf", "rsd0b", "pre0b", "act0a", "rsp0b", "nph",
    "af0a", "cyaf", "dgr0a", "act0b", "dgr0b", "cybf", "ngt0", "zd0", "pre1", "af0b", "zdn0",
    "df0b", "df0a", "npf", "rsp1", "rsd1b", "ya0", "zdq0", "ngt1", "pre2", "cyc", "act1", "dgr1",
    "zd1", "go0", "af1", "gi0", "dact2", "df1", "ya1", "zdn1", "rsp2", "gsi0", "rsd2", "zdq1",
    "act2", "dgr2", "zd2", "dna", "go1", "af2", "gi1", "df2", "ya2", "gsi1", "zdq2", "dnb", "gei0",
    "geo1", "dn2", "geo0", "dp2", "out", "go2", "gi2", "fin", "t3", "gsi2a", "gsi2b", "gb", "lo2",
    "geo2", "gei2a", "gc", "gei1", "gei2b", "gz", "lo3",
)


def rows(start, size, unit=16):
    return pl.ds(pl.multiple_of(start, unit), size)


def kernel(
    tok, gain, win_hbm, wout_hbm, cot,
    layer_out, token_grad, gain_grad, gin_out, gout_out,
    win, wout, nf, ngp, ngt, cg, ab, aq, dg, px, rx1, rx2, po, ro1, ro2, acc, slope,
    pgi, pgo, gi1, gi2, go2, stat, tails, sums, gains, result, wsem_in, wsem_out, osem, rsem_out, ssem, rsem,
):
    d, r, c = lax.axis_index("dp"), lax.axis_index("row"), lax.axis_index("col")
    zh, y = lax.div(d, 4), lax.rem(d, 4)
    zl, co = lax.div(r, 2), lax.rem(r, 2)
    cr, cl = lax.rem(c + 1, 4), lax.rem(c + 3, 4)
    yr, yl = lax.rem(y + 1, 4), lax.rem(y + 3, 4)
    cq, yq = lax.rem(c + 2, 4), lax.rem(y + 2, 4)
    XR, XL, XQ = (d, r, cr), (d, r, cl), (d, r, cq)
    YR, YL, YQ = (zh * 4 + yr, r, c), (zh * 4 + yl, r, c), (zh * 4 + yq, r, c)
    ZL, ZH = (d, (1 - zl) * 2 + co, c), ((1 - zh) * 4 + y, r, c)
    CO, ZLO = (d, zl * 2 + 1 - co, c), (d, (1 - zl) * 2 + 1 - co, c)

    def slot(ref, i, first=0):
        return ref.at[pl.ds(first + 2 * (i % 2), 2), i // 2]

    count = [0]
    sends = []
    V = {"cot": {}}

    def rc(src, dst, dev):
        i = count[0]
        count[0] += 1
        cp = pltpu.make_async_remote_copy(
            src, dst, ssem.at[i], rsem.at[i], device_id=dev, device_id_type=MESH
        )
        cp.start()
        sends.append(cp)
        return cp

    def recv(*cps):
        for cp in cps:
            cp.wait_recv()

    def drain(cps):
        gone = [id(cp) for cp in cps]
        for cp in sends:
            if id(cp) in gone:
                cp.wait_send()
        sends[:] = [cp for cp in sends if id(cp) not in gone]

    barrier = pltpu.get_barrier_semaphore()
    for dev in (XR, XL, XQ, YR, YL, YQ, ZL, ZLO, ZH, CO):
        pl.semaphore_signal(barrier, inc=1, device_id=dev, device_id_type=MESH)

    def place(k):
        return 2 * lax.rem(k, 4) + lax.div(k, 4)

    def win_copy(j, k):
        return pltpu.make_async_copy(
            win_hbm.at[:, rows(k * 384 + j * 128, 128, 128)],
            win.at[j, :, rows(place(k) * 128, 128, 128)],
            wsem_in.at[j, k],
        )

    def wout_copy(j, k):
        return pltpu.make_async_copy(
            wout_hbm.at[rows(k * 384 + j * 128, 128, 128)],
            wout.at[j, rows(place(k) * 128, 128, 128)],
            wsem_out.at[j, k],
        )

    def load(j):
        @pl.loop(0, 8)
        def _(k):
            wout_copy(j, k).start()
            win_copy(j, k).start()

    loaded = []

    def need(copy, key, j):
        if (key, j) not in loaded:
            loaded.append((key, j))

            @pl.loop(0, 8)
            def _(k):
                copy(j, k).wait()

    cg[0, 0:2, 0] = cot[...].reshape(2, HALF, W)
    load(0)
    x = tok[...].astype(F32)
    lane = lax.broadcasted_iota(jnp.int32, (T, 128), 1)

    def two_rows(a, b):
        both = jnp.where(lane == 0, a, jnp.where(lane == 1, b, 0.0))
        both = jnp.concatenate([both, jnp.zeros((128 - T, 128), F32)], axis=0)
        return jnp.transpose(both)[0:8]

    def two_columns(both):
        both = jnp.concatenate([both, jnp.zeros((120, 128), F32)], axis=0)
        return jnp.transpose(both)[0:T]

    stat[0] = two_rows(jnp.sum(x, axis=1, keepdims=True), jnp.sum(x * x, axis=1, keepdims=True))
    pl.semaphore_wait(barrier, 10)

    def mean_inverse():
        mean = sums[0, :, 0:1] / MODEL_WIDTH
        return mean, lax.rsqrt(sums[0, :, 1:2] / MODEL_WIDTH - mean * mean + EPS)

    S = {}

    def spread(key, ref, first=0):
        own = slot(ref, 0, first)
        V[key] = {0: rc(own, slot(ref, 1, first), CO), 1: rc(own, slot(ref, 2, first), ZL)}

    def spread_on(key, ref, first=0):
        recv(V[key][1])
        V[key][2] = rc(slot(ref, 2, first), slot(ref, 3, first), CO)

    done = []

    def once(key, *cps):
        if key not in done:
            done.append(key)
            recv(*cps)

    def own_chip(key):
        once(key + "0", V[key][0])

    def whole(key):
        own_chip(key)
        once(key + "1", V[key][2])

    def cotc():
        V["cot"][0] = rc(slot(cg.at[0], 0), slot(cg.at[0], 1), CO)

    def cotz():
        V["cot"][1] = rc(slot(cg.at[0], 0), slot(cg.at[0], 2), ZL)

    S["cotc"], S["cotz"] = cotc, cotz
    S["cotf"] = lambda: spread_on("cot", cg.at[0])

    def to_column(key, ref):
        V[key] = [rc(ref.at[0], ref.at[1 + i], dev) for i, dev in enumerate((XR, XL, XQ))]

    def of_column(key, ref, i):
        recv(*V[key])
        sums[i] = two_columns((ref[0] + ref[3]) + (ref[1] + ref[2]))

    def st1():
        to_column("sa", stat)
        for j in range(1, NC):
            load(j)

    def st3():
        of_column("sa", stat, 0)
        mean, inverse = mean_inverse()
        normed = ((tok[...].astype(F32) - mean) * inverse * gain[...].reshape(1, W)).astype(BF16)
        nf[0:2, 0] = normed.reshape(2, HALF, W)
        spread("nor", nf)

    S["st1"], S["st3"] = st1, st3
    S["norf"] = lambda: spread_on("nor", nf)

    def norh():
        V["norh"] = rc(
            nf.at[0:2, 0, :, rows((1 - zh) * FG, FG, 128)], slot(ngp, 0), ZH
        )

    def nph():
        recv(V["norh"])
        spread("np", ngp)

    def ngt0():
        whole("nor")
        ngt[:, 0:G] = jnp.transpose(nf[:, :, :, rows(zh * FG, FG, 128)].reshape(G, FG))

    def ngt1():
        whole("np")
        ngt[:, G:] = jnp.transpose(ngp[...].reshape(G, FG))

    S["norh"], S["nph"] = norh, nph
    S["ngt0"], S["ngt1"] = ngt0, ngt1

    def round_y(key, half):
        own = cg.at[0, 0:2, half]
        V[key] = [rc(own, cg.at[3, 0:2, half], YR), rc(own, cg.at[1, 0:2, half], YL)]

    def round_y_on(key, half):
        recv(V[key][0])
        V[key].append(rc(cg.at[3, 0, half], cg.at[2, 0, half], YR))
        recv(V[key][1])
        V[key].append(rc(cg.at[1, 1, half], cg.at[2, 1, half], YL))

    def cyc():
        recv(*V["cya"][2:], *V["cyb"][2:])
        V["cyc"] = rc(cg.at[1:4, 0:2], cg.at[1:4, 2:4], CO)

    S["cya"] = lambda: round_y("cya", 0)
    S["cyaf"] = lambda: round_y_on("cya", 0)
    S["cyb"] = lambda: round_y("cyb", 1)
    S["cybf"] = lambda: round_y_on("cyb", 1)
    S["cyc"] = cyc
    S["npf"] = lambda: spread_on("np", ngp)

    def add(part, buf):
        part[...] = (part[...].astype(F32) + buf[...].astype(F32)).astype(BF16)

    CA, CB = pl.ds(0, H // 2), pl.ds(H // 2, H // 2)

    def product(kind, j, h):
        key = "cot" if kind == 0 else "nor"
        (need(wout_copy, "o", j) if kind == 0 else need(win_copy, "i", j))
        own_chip(key) if h == 0 else whole(key)
        if j >= 2 and h != 1:
            drain(V["x1", kind, j - 2] + V["x2", kind, j - 2])
        src = cg.at[0] if kind == 0 else nf
        part = px.at[kind, j % 2]

        @pl.loop(0, H // 1024)
        def _(n):
            at = rows(n * 1024, 1024, 1024)
            if h is None:
                left = src[...].reshape(G, W)
            else:
                left = src[:, h].reshape(G // 2, W)
            if kind == 0:
                out = lax.dot_general(left, wout[j, at], LAST, preferred_element_type=F32)
            else:
                out = jnp.dot(left, win[j, :, at], preferred_element_type=F32)
            if h is None:
                part[:, :, :, at] = out.astype(BF16).reshape(4, 2, HALF, 1024)
            else:
                part[:, h, :, at] = out.astype(BF16).reshape(4, HALF, 1024)

        buf = rx1.at[kind, j]
        if h is None:
            new = [rc(part.at[cq, 0], buf.at[0], XR), rc(part.at[cq, 1], buf.at[1], XL)]
        else:
            new = [
                rc(part.at[cq, h, :, CA], buf.at[h, :, CA], XR),
                rc(part.at[cq, h, :, CB], buf.at[h, :, CB], XL),
            ]
        V["x1", kind, j, h] = new
        V["x1", kind, j] = V.get(("x1", kind, j), []) + new

    def second(kind, j, h):
        one, other = V["x1", kind, j, h]
        part, buf, out = px.at[kind, j % 2], rx1.at[kind, j], rx2.at[kind, j]
        new = []
        if h is None:
            recv(one)
            add(part.at[cr, 0], buf.at[0])
            new.append(rc(part.at[cr], out.at[0], XR))
            recv(other)
            add(part.at[cl, 1], buf.at[1])
            new.append(rc(part.at[cl], out.at[1], XL))
        else:
            recv(one)
            add(part.at[cr, h, :, CA], buf.at[h, :, CA])
            new.append(rc(part.at[cr, h], out.at[0, h], XR))
            recv(other)
            add(part.at[cl, h, :, CB], buf.at[h, :, CB])
            new.append(rc(part.at[cl, h], out.at[1, h], XL))
        V["x2", kind, j, h] = new
        V["x2", kind, j] = V.get(("x2", kind, j), []) + new

    def total(kind, j, h, at):
        here = slice(None) if h is None else h
        return (
            px[kind, j % 2, c, here, :, at].astype(F32)
            + rx2[kind, j, 0, here, :, at].astype(F32)
            + rx2[kind, j, 1, here, :, at].astype(F32)
        ).reshape(T if h is None else HALF, 256)

    def arrived(kind, j, h):
        split = j in (SPLIT_DACT, SPLIT_PRE)[kind]
        for part in ((0, 1) if h is None else (h,)) if split else (None,):
            once(("x2", kind, j, part), *V["x2", kind, j, part])

    def own_rows(h):
        return rows(c * T, T) if h is None else rows(c * T + h * HALF, HALF)

    def activate(j, h):
        arrived(1, j, h)
        to = slice(0, T) if h is None else slice(h * HALF, (h + 1) * HALF)

        @pl.loop(0, H // 256)
        def _(n):
            at = rows(n * 256, 256, 256)
            pre = total(1, j, h, at)
            cdf = 0.5 * (1.0 + lax.erf(pre * 0.7071067811865476))
            dens = jnp.exp(-0.5 * pre * pre) * 0.3989422804014327
            ab[j, own_rows(h), at] = (pre * cdf).astype(BF16)
            slope[j % 2, to, at] = cdf + pre * dens

        both_ways(("a", j, h), ab.at[j], 0, h)

    def dgelu(j, h):
        arrived(0, j, h)
        to = slice(0, T) if h is None else slice(h * HALF, (h + 1) * HALF)

        @pl.loop(0, H // 256)
        def _(n):
            at = rows(n * 256, 256, 256)
            dg[j, own_rows(h), at] = (total(0, j, h, at) * slope[j % 2, to, at]).astype(BF16)

        both_ways(("d", j, h), dg.at[j], 0, h)

    def both_ways(key, ref, base, h=None):
        own = ref.at[rows(base + c * T, T) if h is None else rows(base + c * T + h * HALF, HALF)]
        V[key] = [rc(own, own, XR), rc(own, own, XL)]

    def forward(key, ref, base, h=None):
        one, other = V[key]
        once((key, 0), one)
        if h is None:
            a = ref.at[rows(base + cl * T, HALF)]
            b = ref.at[rows(base + cr * T + HALF, HALF)]
        else:
            a = ref.at[rows(base + cl * T + h * HALF, HALF), CA]
            b = ref.at[rows(base + cr * T + h * HALF, HALF), CB]
        V[key].append(rc(a, a, XR))
        once((key, 1), other)
        V[key].append(rc(b, b, XL))

    def ends(key):
        once((key, 2), V[key][2])
        once((key, 3), V[key][3])

    def halves(j):
        return ((0, "a"), (1, "b")) if j in SPLIT_ACT else ((None, ""),)

    def all_ends(kind, j):
        for h, _ in halves(j):
            ends((kind, j, h))

    def over_z(j, piece):
        return rc(dg.at[j, rows(piece * T, T)], dg.at[j, rows(G + piece * T, T)], ZH)

    def partner_steps(j, way):
        key = ("dp", j)

        def z_own():
            V["z", j] = over_z(j, c)

        S["zd%d" % j] = z_own

        def over_x():
            once(("z", j), V["z", j])
            both_ways(key, dg.at[j], G)

        def opposite():
            all_ends("d", j)
            V["zq", j] = over_z(j, cq)

        def neighbours():
            for h, _ in halves(j):
                for i in (0, 1):
                    once((("d", j, h), i), V["d", j, h][i])
            V["zn", j] = [over_z(j, cl), over_z(j, cr)]

        if way < 4:
            S["dp%d" % j] = over_x
        if way == 1:
            S["dpf%d" % j] = lambda: forward(key, dg.at[j], G)
        if way > 1:
            S["zdq%d" % j] = opposite
        if way == 4:
            S["zdn%d" % j] = neighbours

        def wait():
            if way == 1:
                ends(key)
            elif way == 2:
                recv(*V[key], V["zq", j])
            else:
                recv(V["z", j], *V["zn", j], V["zq", j])

        return wait

    ocps = []

    def out_copy(key, j, k):
        if key == "o":
            return pltpu.make_async_copy(
                pgo.at[j, 1], gout_out.at[0, pl.ds(j * 128, 128)], osem.at[0, j, 0]
            )
        return pltpu.make_async_copy(
            gi2.at[j, 0, :, pl.ds((2 * (k % 4) + k // 4) * 128, 128)],
            gin_out.at[0, :, pl.ds(k * 384 + j * 128, 128)],
            osem.at[1, j, k],
        )

    def grad_out_steps(j):
        def spread_act():
            all_ends("a", j)
            V["ya", j] = [
                rc(ab.at[j, :, rows(to * 256, 256, 256)], aq.at[j, i], dev)
                for to, i, dev in ((yr, 3, YR), (yl, 1, YL), (yq, 2, YQ))
            ]

        def block(z):
            at = rows(z * 128, 128, 128)
            return lax.dot_general(
                aq[j, :, :, at].reshape(4 * G, 128),
                cg[...].reshape(4 * G, W),
                FIRST,
                preferred_element_type=F32,
            ).astype(BF16)

        def compute():
            all_ends("a", j)
            aq[j, 0] = ab[j, :, rows(y * 256, 256, 256)]
            recv(*V["ya", j])
            once("cyc", V["cyc"])
            pgo[j, 0] = block(1 - zh)
            V["o", j] = rc(pgo.at[j, 0], go2.at[j], ZH)
            pgo[j, 1] = block(zh)

        def end():
            recv(V["o", j])
            add(pgo.at[j, 1], go2.at[j])
            cp = out_copy("o", j, 0)
            cp.start()
            ocps.append(cp)

        S["ya%d" % j], S["go%d" % j], S["geo%d" % j] = spread_act, compute, end

    def gradient_steps(key, j, wait, split):
        part, b1, b2, size = pgi.at[j % 2], gi1.at[j], gi2.at[j], FB
        pieces = (("a", 0), ("b", 1)) if split else (("", 0),)
        ps = size // len(pieces)
        h = ps // 2

        def block(b):
            at = rows(b * size, size)
            part[at] = jnp.dot(ngt[at], dg[j], preferred_element_type=F32).astype(BF16)

        def compute():
            all_ends("d", j)
            wait()
            if j >= 2:
                drain(V["y", key, j - 2])
            block(yq)
            V["y", key, j] = []
            for name, p in pieces:
                new = [
                    rc(part.at[rows(yq * size + p * ps, h)], b1.at[rows(2 * p * h, h)], YR),
                    rc(part.at[rows(yq * size + p * ps + h, h)], b1.at[rows(2 * p * h + h, h)], YL),
                ]
                V["y1", key, j, name] = new
                V["y", key, j] += new

            @pl.loop(1, 4)
            def _(i):
                block(lax.rem(yq + i, 4))

        S["g%s%d" % (key, j)] = compute

        def piece_steps(name, p):
            def on():
                one, other = V["y1", key, j, name]
                recv(one)
                add(part.at[rows(yr * size + p * ps, h)], b1.at[rows(2 * p * h, h)])
                new = [rc(part.at[rows(yr * size + p * ps, ps)], b2.at[0, rows(p * ps, ps)], YR)]
                recv(other)
                add(part.at[rows(yl * size + p * ps + h, h)], b1.at[rows(2 * p * h + h, h)])
                new.append(rc(part.at[rows(yl * size + p * ps, ps)], b2.at[1, rows(p * ps, ps)], YL))
                V["y2", key, j, name] = new
                V["y", key, j] += new

            def end():
                recv(*V["y2", key, j, name])
                at = rows(p * ps, ps)
                b2[0, at] = (
                    part[rows(y * size + p * ps, ps)].astype(F32)
                    + b2[0, at].astype(F32)
                    + b2[1, at].astype(F32)
                ).astype(BF16)
                V["left", key, j] = V.get(("left", key, j), len(pieces)) - 1
                if V["left", key, j] == 0:
                    for k in range(8):
                        cp = out_copy(key, j, k)
                        cp.start()
                        ocps.append(cp)

            S["gs%s%d%s" % (key, j, name)] = on
            S["ge%s%d%s" % (key, j, name)] = end

        for name, p in pieces:
            piece_steps(name, p)

    def chunk_steps(j):
        for kind, name, k, split in (
            (0, "dact", "d", j in SPLIT_DACT),
            (1, "pre", "p", j in SPLIT_PRE),
        ):
            for h, tail in ((0, "a"), (1, "b")) if split else ((None, ""),):
                S["%s%d%s" % (name, j, tail)] = lambda kind=kind, h=h: product(kind, j, h)
                S["rs%s%d%s" % (k, j, tail)] = lambda kind=kind, h=h: second(kind, j, h)
        for h, tail in halves(j):
            S["act%d%s" % (j, tail)] = lambda h=h: activate(j, h)
            S["dgr%d%s" % (j, tail)] = lambda h=h: dgelu(j, h)
            S["af%d%s" % (j, tail)] = lambda h=h: forward(("a", j, h), ab.at[j], 0, h)
            S["df%d%s" % (j, tail)] = lambda h=h: forward(("d", j, h), dg.at[j], 0, h)
        grad_out_steps(j)
        gradient_steps("i", j, partner_steps(j, DPRE_WAY[j]), j in SPLIT_IN)

    for j in range(NC):
        chunk_steps(j)

    def out():
        for j in range(NC):
            all_ends("a", j)

        @pl.loop(0, W // 768)
        def _(n):
            at = rows(n * 768, 768, 768)
            total = jnp.dot(ab[0], wout[0, :, at], preferred_element_type=F32)
            for j in range(1, NC):
                total += jnp.dot(ab[j], wout[j, :, at], preferred_element_type=F32)
            po[0, :, :, :, at] = total.astype(BF16).reshape(4, 2, HALF, 768)

        V["lo1"] = rc(po.at[0, 2:4], ro1.at[0], CO)

    def dna():
        for j in (0, 1):
            all_ends("d", j)

        @pl.loop(0, W // 768)
        def _(n):
            at = rows(n * 768, 768, 768)
            acc[:, at] = sum(
                lax.dot_general(dg[j, 0:G], win[j, at], LAST, preferred_element_type=F32)
                for j in (0, 1)
            )

    def dnb():
        all_ends("d", 2)

        @pl.loop(0, W // 768)
        def _(n):
            at = rows(n * 768, 768, 768)
            total = acc[:, at] + lax.dot_general(
                dg[2, 0:G], win[2, at], LAST, preferred_element_type=F32
            )
            po[1, :, :, :, at] = total.astype(BF16).reshape(4, 2, HALF, 768)

        V["dn1"] = rc(po.at[1, 2:4], ro1.at[1], CO)

    def row_second(q, key):
        recv(V[key])
        add(po.at[q, 0:2, 1], ro1.at[q, :, 1])
        return rc(po.at[q, 0:2, 1], ro2.at[q], ZL)

    def row_sum(q):
        return (
            po[q, 0:2, 0].astype(F32) + ro1[q, :, 0].astype(F32) + ro2[q].astype(F32)
        ).reshape(T, W)

    def lo2():
        V["lo2"] = row_second(0, "lo1")

    def dn2():
        V["dn2"] = row_second(1, "dn1")

    def leave(i, out):
        cp = pltpu.make_async_copy(result.at[i], out, rsem_out.at[i])
        cp.start()
        ocps.append(cp)

    def lo3():
        recv(V["lo2"])
        result[0] = (tok[...].astype(F32) + row_sum(0)).astype(BF16)
        leave(0, layer_out)

    def fin():
        recv(V["dn2"])
        mean, inverse = mean_inverse()
        dnorm = row_sum(1)
        xhat = (tok[...].astype(F32) - mean) * inverse
        gains[r] = jnp.sum(dnorm * xhat, axis=0, keepdims=True)
        V["ga"] = [rc(gains.at[r], gains.at[r], dev) for dev in (CO, ZL, ZLO)]
        dxhat = dnorm * gain[...].reshape(1, W)
        tails[0] = two_rows(
            jnp.sum(dxhat, axis=1, keepdims=True), jnp.sum(dxhat * xhat, axis=1, keepdims=True)
        )
        to_column("ta", tails)

    def t3():
        of_column("ta", tails, 1)
        mean, inverse = mean_inverse()
        first = sums[1, :, 0:1] / MODEL_WIDTH
        second = sums[1, :, 1:2] / MODEL_WIDTH
        xhat = (tok[...].astype(F32) - mean) * inverse
        result[1] = (
            cot[...].astype(F32) + inverse * (row_sum(1) * gain[...].reshape(1, W) - first - xhat * second)
        ).astype(BF16)
        leave(1, token_grad)

    def gb():
        recv(*V["ga"])
        gains[4 + zh] = (gains[0] + gains[1]) + (gains[2] + gains[3])
        V["gb"] = rc(gains.at[4 + zh], gains.at[4 + zh], ZH)

    def gc():
        recv(V["gb"])
        gains[6 + y] = gains[4] + gains[5]
        V["gc"] = [rc(gains.at[6 + y], gains.at[6 + y], dev) for dev in (YR, YL, YQ)]

    def gz():
        recv(*V["gc"])
        gain_grad[...] = jnp.sum((gains[6] + gains[7]) + (gains[8] + gains[9]), axis=0)

    S.update(out=out, dna=dna, dnb=dnb, lo2=lo2, dn2=dn2, lo3=lo3, fin=fin, t3=t3, gz=gz)
    S["gb"], S["gc"] = gb, gc

    assert sorted(S) == sorted(ORDER)
    for i, name in enumerate(ORDER):
        if i >= len(ORDER) - 12:
            drain(sends[:-16])
        S[name]()
    drain(list(sends))
    for cp in ocps:
        cp.wait()
    assert count[0] <= N_COPIES, count[0]


N_COPIES = 230


def parts(i, ref):
    if i < 3:
        return [ref]
    n = ref.shape[1] // 4
    return [ref.at[0, pl.ds(k * n, n)] for k in range(4)]


def copy_kernel(*refs):
    src, dst, via, (one, two) = refs[:5], refs[5:10], refs[10:15], refs[15:]
    moves = []
    for i in (3, 4, 0, 1, 2):
        moves += list(zip(parts(i, src[i]), parts(i, via[i]), parts(i, dst[i])))
    first = [pltpu.make_async_copy(a, v, one.at[k]) for k, (a, v, _) in enumerate(moves)]
    then = [pltpu.make_async_copy(v, b, two.at[k]) for k, (_, v, b) in enumerate(moves)]
    for cp in first:
        cp.start()
    for a, b in zip(first, then):
        a.wait()
        b.start()
    for cp in then:
        cp.wait()


def body(tokens, norm_scale_gain, in_weight, out_weight, cotangent):
    vm = pl.BlockSpec(memory_space=pltpu.VMEM)
    hbm = pl.BlockSpec(memory_space=pl.ANY)
    layer_out, token_grad, gain_grad, grad_in, grad_out = pl.pallas_call(
        kernel,
        out_shape=(
            jax.ShapeDtypeStruct((T, W), BF16),
            jax.ShapeDtypeStruct((T, W), BF16),
            jax.ShapeDtypeStruct((W,), F32),
            jax.ShapeDtypeStruct((1, FB, NC * H), BF16),
            jax.ShapeDtypeStruct((1, NC * 128, W), BF16),
        ),
        in_specs=[vm, vm, hbm, hbm, vm],
        out_specs=(hbm, hbm, vm, hbm, hbm),
        scratch_shapes=[
            pltpu.VMEM((NC, W, H), BF16),
            pltpu.VMEM((NC, H, W), BF16),
            pltpu.VMEM((4, 2, HALF, W), BF16),
            pltpu.VMEM((4, 2, HALF, FG), BF16),
            pltpu.VMEM((FG, 2 * G), BF16),
            pltpu.VMEM((4, 4, 2, HALF, W), BF16),
            pltpu.VMEM((NC, G, H), BF16),
            pltpu.VMEM((NC, 4, G, 256), BF16),
            pltpu.VMEM((NC, 2 * G, H), BF16),
            pltpu.VMEM((2, 2, 4, 2, HALF, H), BF16),
            pltpu.VMEM((2, NC, 2, HALF, H), BF16),
            pltpu.VMEM((2, NC, 2, 2, HALF, H), BF16),
            pltpu.VMEM((2, 4, 2, HALF, W), BF16),
            pltpu.VMEM((2, 2, 2, HALF, W), BF16),
            pltpu.VMEM((2, 2, HALF, W), BF16),
            pltpu.VMEM((G, W), F32),
            pltpu.VMEM((2, T, H), F32),
            pltpu.VMEM((2, FG, H), BF16),
            pltpu.VMEM((NC, 2, 128, W), BF16),
            pltpu.VMEM((NC, FB, H), BF16),
            pltpu.VMEM((NC, 2, FB, H), BF16),
            pltpu.VMEM((NC, 128, W), BF16),
            pltpu.VMEM((4, 8, 128), F32),
            pltpu.VMEM((4, 8, 128), F32),
            pltpu.VMEM((2, T, 128), F32),
            pltpu.VMEM((10, 1, W), F32),
            pltpu.VMEM((2, T, W), BF16),
            pltpu.SemaphoreType.DMA((NC, 8)),
            pltpu.SemaphoreType.DMA((NC, 8)),
            pltpu.SemaphoreType.DMA((2, NC, 8)),
            pltpu.SemaphoreType.DMA((2,)),
            pltpu.SemaphoreType.DMA((N_COPIES,)),
            pltpu.SemaphoreType.DMA((N_COPIES,)),
        ],
        compiler_params=pltpu.CompilerParams(
            collective_id=0, has_side_effects=True, vmem_limit_bytes=63 * 2**20
        ),
        cost_estimate=pl.CostEstimate(
            flops=22 * 10**9, bytes_accessed=24 * 10**6, transcendentals=600000
        ),
        name="feed_forward",
    )(tokens, norm_scale_gain, in_weight, out_weight, cotangent)
    arrays = (layer_out, token_grad, gain_grad, grad_in, grad_out)
    return pl.pallas_call(
        copy_kernel,
        out_shape=tuple(jax.ShapeDtypeStruct(a.shape, a.dtype) for a in arrays),
        in_specs=[hbm] * 5,
        out_specs=(hbm,) * 5,
        scratch_shapes=[pltpu.VMEM(a.shape, a.dtype) for a in arrays]
        + [pltpu.SemaphoreType.DMA((11,)), pltpu.SemaphoreType.DMA((11,))],
        name="results",
    )(*arrays)


def solution(mesh):
    in_specs = (
        P(("dp", "row"), "col"),
        P("col"),
        P("col", "row"),
        P("row", "col"),
        P(("dp", "row"), "col"),
    )
    out_specs = (
        P(("dp", "row"), "col"),
        P(("dp", "row"), "col"),
        P("col"),
        P("dp", "col", "row"),
        P("dp", "row", "col"),
    )
    return jax.shard_map(body, mesh=mesh, in_specs=in_specs, out_specs=out_specs, check_vma=False)
```
